256 devices in a mesh: ctx: 32 (over z, y_lo, core), tp: 8 (over x, y_hi).
Axes of the slice: x: 4, y: 4 (y_hi: 2, y_lo: 2; y = y_hi * 2 + y_lo), z: 8, core: 2. Of those that a mesh axis runs over, the one named last changes fastest.
Arguments:
- tokens: bfloat16 [16384, 4096], P('ctx', 'tp'), may hold values from -6 to 6
- w_in: bfloat16 [3, 4096, 4096], P(None, 'ctx', 'tp'), may hold values from -0.09375 to 0.09375
- short_taps: float32 [3, 4096, 3], P(None, 'tp'), may hold values from -3 to 3
- filters: bfloat16 [256, 16384], P('tp', 'ctx'), may hold values from 0 to 0.5
- skip: float32 [4096], P('tp'), may hold values from 0.5 to 1.5
- w_out: bfloat16 [4096, 4096], P('tp', 'ctx'), may hold values from -0.09375 to 0.09375
Outputs:
- mixed: bfloat16 [16384, 4096], P('ctx', 'tp')
The draws below stay inside these ranges and needn't reach their ends.
All inputs are finite; a program needn't handle non-finite values.
Results may differ from the reference program's by a relative error of at most 0.015.
Values may be sent and summed in bfloat16 or wider, within the bound.
No kernel may reach another device: no remote copies, remote signals or barrier semaphores. Data moves between devices by JAX's collectives and lax.ppermute only.
A program may use at most 64 MiB of HBM per device.

```python
import math
import jax
import jax.numpy as jnp
from jax import lax

D_IN = 4096
CHAN = 4096
D_OUT = 4096
GROUP = 16
TAPS = 3
GENOME_LENGTH = 16384
N_TP = 8


def draw_filters(key, part):
    key = jax.random.fold_in(key, 7)
    rate_key, rough_key, mark_key = jax.random.split(key, 3)
    source_matrix_lines = CHAN // GROUP
    attenuation_factors = jnp.exp(jax.random.uniform(rate_key, (source_matrix_lines, 1), jnp.float32, math.log(0.3 / GENOME_LENGTH), math.log(1.0 / 30.0)))
    genome_moments = jnp.arange(GENOME_LENGTH).astype(jnp.float32)[None, :]
    trace_strength = jnp.sqrt(jnp.maximum(2.0 * attenuation_factors, 1.0 / GENOME_LENGTH))
    jittered_trace = jax.random.uniform(rough_key, (source_matrix_lines, GENOME_LENGTH), jnp.float32, 0.4, 1.6)
    highlighted_sites_list = jax.random.randint(mark_key, (source_matrix_lines, 3), 0, GENOME_LENGTH).astype(jnp.float32)
    kick_group_response = jnp.ones((source_matrix_lines, GENOME_LENGTH), jnp.float32)
    for picked_entry_place in range(3):
        kick_group_response = kick_group_response * jnp.where(genome_moments >= highlighted_sites_list[:, picked_entry_place:picked_entry_place + 1], 0.6, 1.0)
    carried_items = trace_strength * jnp.exp(-attenuation_factors * genome_moments) * jittered_trace * kick_group_response
    return carried_items.astype(jnp.bfloat16)


def levels(stream_key, shape, pieces, smallest, high):
    level, own = 1.0, jax.random.fold_in(stream_key, 6)
    for dim, parts in pieces:
        steps = jnp.exp(jax.random.uniform(jax.random.fold_in(own, dim), (parts,), jnp.float32, smallest / len(pieces), high / len(pieces)))
        level = level * jnp.repeat(steps, shape[dim] // parts).reshape([-1 if axis == dim else 1 for axis in range(len(shape))])
    return level


def centred(own_key, shape, spread, bound, cuts=(), held_as=jnp.bfloat16):
    values = spread * jax.random.normal(own_key, shape, jnp.float32)
    if cuts:
        values = values * levels(own_key, shape, cuts, -0.22, 0.18)
    return jnp.clip(values, -bound, bound).astype(held_as)


def setup_inputs(seed: int = 0) -> dict:
    arg_keys = jax.random.split(jax.random.key(seed), 7)
    tokens = centred(arg_keys[0], (GENOME_LENGTH, D_IN), 1.0, 6.0, ((0, 32), (1, 8)))
    w_in = centred(arg_keys[1], (3, D_IN, CHAN), D_IN ** -0.5, 0.09375, ((1, 32), (2, 8)))
    short_taps = centred(arg_keys[2], (3, CHAN, TAPS), 0.6, 3.0, ((1, 8),), jnp.float32)
    filters = draw_filters(jax.random.fold_in(arg_keys[6], 71), 0)
    skip = jnp.clip(0.5 + 1.0 * jax.random.uniform(arg_keys[4], (CHAN,), jnp.float32) ** levels(arg_keys[4], (CHAN,), ((0, 8),), -0.2, 0.2), 0.5, 1.5)
    w_out = centred(arg_keys[5], (CHAN, D_OUT), CHAN ** -0.5, 0.09375, ((0, 8), (1, 32)))
    return {"tokens": tokens, "w_in": w_in, "short_taps": short_taps, "filters": filters, "skip": skip, "w_out": w_out}


def reference(tokens, w_in, short_taps, filters, skip, w_out):
    projections = []
    for picked_entry_place in range(3):
        product = jnp.dot(tokens, w_in[picked_entry_place], preferred_element_type=jnp.float32)
        projections.append(product.astype(jnp.bfloat16).T)
    projected = jnp.stack(projections)
    widened = jnp.pad(projected.astype(jnp.float32), ((0, 0), (0, 0), (TAPS - 1, 0)))
    smoothed = jnp.zeros(projected.shape, jnp.float32)
    for lag in range(TAPS):
        smoothed = smoothed + short_taps[:, :, lag:lag + 1] * widened[:, :, TAPS - 1 - lag:TAPS - 1 - lag + GENOME_LENGTH]
    query_gate = smoothed[0]
    key_gate = smoothed[1]
    value_part = smoothed[2]
    mixed_in = (key_gate * value_part).astype(jnp.bfloat16)
    group_width = math.gcd(CHAN, 256)
    group_count = CHAN // group_width

    def convolve(pair):
        signal = pair[0].astype(jnp.float32)
        kernel = jnp.repeat(pair[1].astype(jnp.float32), GROUP, axis=0)
        spectrum = jnp.fft.rfft(signal, n=2 * GENOME_LENGTH, axis=-1) * jnp.fft.rfft(kernel, n=2 * GENOME_LENGTH, axis=-1)
        result = jnp.fft.irfft(spectrum, n=2 * GENOME_LENGTH, axis=-1)[:, :GENOME_LENGTH]
        return result.astype(jnp.bfloat16)

    conv = lax.map(convolve, (mixed_in.reshape(group_count, group_width, GENOME_LENGTH),
                              filters.reshape(group_count, group_width // GROUP, GENOME_LENGTH)))
    conv = conv.reshape(CHAN, GENOME_LENGTH)
    gated = (query_gate * (conv.astype(jnp.float32) + skip[:, None] * mixed_in.astype(jnp.float32))).astype(jnp.bfloat16)
    span_width = CHAN // N_TP
    gated_groups = gated.reshape(N_TP, span_width, GENOME_LENGTH)
    weight_groups = w_out.reshape(N_TP, span_width, D_OUT)

    def add_group(total, pair):
        partial_sum = jnp.dot(pair[0].T, pair[1], preferred_element_type=jnp.float32)
        rounded = lax.optimization_barrier(partial_sum.astype(jnp.bfloat16))
        return total + rounded.astype(jnp.float32), None

    total, unused = lax.scan(add_group, jnp.zeros((GENOME_LENGTH, D_OUT), jnp.float32), (gated_groups, weight_groups))
    return total.astype(jnp.bfloat16)
```

```python
import functools

import jax
import jax.numpy as jnp
from jax import lax
from jax.experimental import pallas as pl
from jax.experimental.pallas import tpu as pltpu
from jax.sharding import PartitionSpec as P

F32 = jnp.float32
BF16 = jnp.bfloat16
ANY = pl.BlockSpec(memory_space=pl.ANY)
VMEM = pl.BlockSpec(memory_space=pltpu.VMEM)
VMEM_LIMIT = 48 * 1024 * 1024

NZ, NX = 8, 4
CTX = NZ * 4
TP = NX * 2
TAIL = 16


def barrier(*arrays):
    return lax.optimization_barrier(arrays)


def shift_z(block, step):
    route = [(i, (i + 4 * step) % CTX) for i in range(CTX)]
    return lax.ppermute(block, "ctx", route)


def swap_ctx(block, mask):
    return lax.ppermute(block, "ctx", [(i, i ^ mask) for i in range(CTX)])


def swap_core(block):
    return swap_ctx(block, 1)


def swap_ylo(block):
    return swap_ctx(block, 2)


def shift_x(block, step):
    route = [(j, (j + 2 * step) % TP) for j in range(TP)]
    return lax.ppermute(block, "tp", route)


def swap_yhi(block):
    return lax.ppermute(block, "tp", [(j, j ^ 1) for j in range(TP)])


def gather_z(block):
    groups = [[4 * z + rest for z in range(NZ)] for rest in range(4)]
    return lax.all_gather(block, "ctx", axis=0, tiled=False, axis_index_groups=groups)


def gather_tp(own):
    rows = own.shape[0]
    half = rows // 2
    near = swap_yhi(own)
    own_right, own_left = shift_x(own, 1), shift_x(own, -1)
    near_right, near_left = shift_x(near, 1), shift_x(near, -1)
    far_right = shift_x(jnp.concatenate([own_right[:half], near_right[:half]]), 1)
    far_left = shift_x(jnp.concatenate([own_left[half:], near_left[half:]]), -1)
    return [own, near, own_right, own_left, near_right, near_left, far_right, far_left]


def piece_copies(pieces, dst, first_row, sem):
    me = lax.axis_index("tp")
    x, y = me // 2, me % 2
    width = pieces[0].shape[1]
    rows = pieces[0].shape[0]
    half = rows // 2

    def place(dx, dy, begin, count):
        there = ((x + dx + NX) % NX) * 2 + (y + dy) % 2
        lanes = pl.ds(pl.multiple_of(there * width, width), width)
        return dst.at[pl.ds(first_row + begin, count), lanes]

    whole = [(0, 0), (0, 1), (-1, 0), (1, 0), (-1, 1), (1, 1)]
    copies = []
    for ref, (dx, dy) in zip(pieces[:6], whole):
        copies.append((ref, place(dx, dy, 0, rows)))
    for ref, begin in ((pieces[6], 0), (pieces[7], half)):
        for dy in (0, 1):
            copies.append((ref.at[pl.ds(dy * half, half)], place(2, dy, begin, half)))
    return [pltpu.make_async_copy(src, to, sem) for src, to in copies]


def weight_slots():
    me = lax.axis_index("ctx")
    return (me // 2) % 2, me % 2


def project_kernel(n_proj, width, *refs):
    pieces = refs[:8]
    tail, mine, other, taps = refs[8:12]
    outs = refs[12:-6]
    tok, wts, part, tok_sem, tail_sem, w_sems = refs[-6:]
    rows = pieces[0].shape[0]
    total = wts.shape[3]
    chan = total // n_proj
    n_tiles = chan // width
    y, core = weight_slots()

    copies = piece_copies(pieces, tok, TAIL, tok_sem)
    for j in range(TP):
        copies.append(
            pltpu.make_async_copy(tail.at[j], tok.at[pl.ds(0, TAIL), pl.ds(j * 512, 512)], tail_sem)
        )
    for copy in copies:
        copy.start()
    w_copies = []
    for tile in range(n_tiles):
        group = []
        for proj in range(n_proj):
            lanes = pl.ds(proj * chan + tile * width, width)
            for ref, dc in ((mine, 0), (other, 1)):
                for dy in (0, 1):
                    slot = ((y + dy) % 2) * 2 + (core + dc) % 2
                    group.append(
                        pltpu.make_async_copy(
                            ref.at[:, dy, :, lanes], wts.at[:, slot, :, lanes], w_sems.at[tile]
                        )
                    )
        for copy in group:
            copy.start()
        w_copies.append(group)
    for copy in copies:
        copy.wait()
    for tile in range(n_tiles):
        for copy in w_copies[tile]:
            copy.wait()
        smooth = []
        for proj in range(n_proj):
            lanes = pl.ds(proj * chan + tile * width, width)
            weights = wts[:, :, :, lanes].reshape(-1, width)
            product = jnp.dot(tok[...], weights, preferred_element_type=F32)
            part[proj] = product.astype(BF16).astype(F32)
            cols = pl.ds(tile * width, width)
            value = taps[proj, 0:1, cols] * part[proj, pl.ds(TAIL, rows), :]
            value = value + taps[proj, 1:2, cols] * part[proj, pl.ds(TAIL - 1, rows), :]
            value = value + taps[proj, 2:3, cols] * part[proj, pl.ds(TAIL - 2, rows), :]
            smooth.append(value)
        cols = pl.ds(tile * width, width)
        if n_proj == 1:
            outs[0][:, cols] = smooth[0]
        else:
            mixed = smooth[0] * smooth[1]
            outs[0][:, cols] = mixed.astype(BF16)
            turned = mixed.T.astype(BF16)
            for a in range(2):
                block = turned[:, 256 * a : 256 * a + 256].reshape(width // 16, 16, 256)
                outs[1][pl.ds(tile * (width // 16), width // 16), pl.ds(16 * a, 16), :] = block


def project(pieces, tail, mine, other, taps, out_shapes):
    n_proj = taps.shape[0]
    total = mine.shape[-1]
    width = 256
    n_tiles = total // n_proj // width
    rows = pieces[0].shape[0]
    depth = TP * pieces[0].shape[1]
    return pl.pallas_call(
        functools.partial(project_kernel, n_proj, width),
        out_shape=out_shapes,
        in_specs=[ANY] * 8 + [ANY, ANY, ANY, VMEM],
        out_specs=[VMEM] * len(out_shapes),
        scratch_shapes=[
            pltpu.VMEM((TAIL + rows, depth), BF16),
            pltpu.VMEM((NZ, 4, depth // CTX, total), BF16),
            pltpu.VMEM((n_proj, TAIL + rows, width), F32),
            pltpu.SemaphoreType.DMA,
            pltpu.SemaphoreType.DMA,
            pltpu.SemaphoreType.DMA((n_tiles,)),
        ],
        compiler_params=pltpu.CompilerParams(vmem_limit_bytes=VMEM_LIMIT),
        name="project%d" % n_proj,
    )(*pieces, tail, mine, other, taps)


def toeplitz_kernel(seg_ref, out_ref):
    low = lax.broadcasted_iota(jnp.int32, (128, 128), 1) >= lax.broadcasted_iota(
        jnp.int32, (128, 128), 0
    )

    def turn(m):
        row = jnp.broadcast_to(seg_ref[pl.ds(m, 1), :], (128, 128))
        return pltpu.roll(row, 0, 1, stride=1, stride_axis=0)

    def body(d, before):
        even = turn(2 * d)
        odd = turn(2 * d + 1)
        first = jnp.where(low, even, before).astype(BF16)
        second = jnp.where(low, odd, even).astype(BF16)
        out_ref[d, 0:128, 0:128] = first
        out_ref[d, 128:256, 128:256] = first
        out_ref[d, 0:128, 128:256] = second

        @pl.when(d < 63)
        def _():
            out_ref[d + 1, 128:256, 0:128] = second

        return odd

    out_ref[0, 128:256, 0:128] = jnp.zeros((128, 128), BF16)
    lax.fori_loop(0, 64, body, jnp.zeros((128, 128), F32))


def toeplitz(segments):
    return pl.pallas_call(
        toeplitz_kernel,
        out_shape=jax.ShapeDtypeStruct((64, 256, 256), BF16),
        in_specs=[VMEM],
        out_specs=VMEM,
        compiler_params=pltpu.CompilerParams(vmem_limit_bytes=VMEM_LIMIT),
        name="toeplitz",
    )(segments)


FOLD = 4


def conv_kernel(x_ref, h_hbm, y_ref, wide, acc, h_ref, sems):
    rows = x_ref.shape[0]
    steps = h_ref.shape[0]
    copies = [pltpu.make_async_copy(h_hbm.at[g], h_ref.at[g], sems.at[g]) for g in range(steps)]
    for copy in copies:
        copy.start()
    for k in range(FOLD):
        if k:
            wide[0 : 16 * k, 256 * k : 256 * k + 256] = jnp.zeros((16 * k, 256), BF16)
        wide[16 * k : rows, 256 * k : 256 * k + 256] = x_ref[0 : rows - 16 * k, :]
    for g in range(steps):
        copies[g].wait()
        skip = 16 * FOLD * g
        product = jnp.dot(wide[0 : rows - skip, :], h_ref[g], preferred_element_type=F32)
        if g == 0:
            acc[...] = product
        else:
            acc[skip:rows, :] += product
    y_ref[...] = acc[...].astype(BF16)


def conv(x, table):
    rows = x.shape[0]
    steps = 64 // FOLD
    return pl.pallas_call(
        conv_kernel,
        out_shape=jax.ShapeDtypeStruct((rows, 256), BF16),
        in_specs=[VMEM, ANY],
        out_specs=VMEM,
        scratch_shapes=[
            pltpu.VMEM((rows, FOLD * 256), BF16),
            pltpu.VMEM((rows, 256), F32),
            pltpu.VMEM((steps, FOLD * 256, 256), BF16),
            pltpu.SemaphoreType.DMA((steps,)),
        ],
        compiler_params=pltpu.CompilerParams(vmem_limit_bytes=VMEM_LIMIT),
        name="conv",
    )(x, table.reshape(steps, FOLD * 256, 256))


def gate_kernel(back_ref, mixed_ref, query_ref, skip_ref, out_ref):
    chan = mixed_ref.shape[1]
    for a in range(2):
        block = back_ref[:, 16 * a : 16 * a + 16, :].reshape(chan, 256)
        turned = block.astype(F32).T
        here = pl.ds(256 * a, 256)
        mixed = mixed_ref[here, :].astype(F32)
        out_ref[here, :] = (query_ref[here, :] * (turned + skip_ref[...] * mixed)).astype(BF16)


def gate(back, mixed, query, skip):
    return pl.pallas_call(
        gate_kernel,
        out_shape=jax.ShapeDtypeStruct(mixed.shape, BF16),
        in_specs=[VMEM] * 4,
        out_specs=VMEM,
        compiler_params=pltpu.CompilerParams(vmem_limit_bytes=VMEM_LIMIT),
        name="gate",
    )(back, mixed, query, skip)


def output_kernel(*refs):
    pieces = refs[:8]
    mine, other, out_ref, act, wts, act_sem, w_sem = refs[8:]
    y, core = weight_slots()
    copies = piece_copies(pieces, act, 0, act_sem)
    depth, width = mine.shape[2:]
    for ref, dc in ((mine, 0), (other, 1)):
        for dy in (0, 1):
            slot = ((y + dy) % 2) * 2 + (core + dc) % 2
            lanes = pl.ds(pl.multiple_of(slot * width, width), width)
            copies.append(pltpu.make_async_copy(ref.at[:, dy], wts.at[:, :, lanes], w_sem))
    for copy in copies:
        copy.start()
    for copy in copies:
        copy.wait()
    weights = wts[...].reshape(-1, wts.shape[2])
    out_ref[...] = jnp.dot(act[...], weights, preferred_element_type=F32).astype(BF16)


def output(pieces, mine, other):
    rows, part = pieces[0].shape
    depth, width = mine.shape[2:]
    return pl.pallas_call(
        output_kernel,
        out_shape=jax.ShapeDtypeStruct((rows, 4 * width), BF16),
        in_specs=[ANY] * 10,
        out_specs=VMEM,
        scratch_shapes=[
            pltpu.VMEM((rows, TP * part), BF16),
            pltpu.VMEM((NZ, depth, 4 * width), BF16),
            pltpu.SemaphoreType.DMA,
            pltpu.SemaphoreType.DMA,
        ],
        compiler_params=pltpu.CompilerParams(vmem_limit_bytes=VMEM_LIMIT),
        name="output",
    )(*pieces, mine, other)


def gather_weights(block):
    pair = jnp.stack([block, swap_ylo(block)])
    mine = gather_z(pair)
    return mine, swap_core(mine)


def local(tokens, w_in, short_taps, filters, skip, w_out):
    rows, _ = tokens.shape
    chan = w_in.shape[2]
    taps = short_taps.transpose(0, 2, 1)

    kv = jnp.concatenate([w_in[1], w_in[2]], axis=1)
    kv_mine, kv_other = gather_weights(kv)

    before = lax.ppermute(tokens[rows - TAIL :], "ctx", [(i, i + 1) for i in range(CTX - 1)])
    pieces = gather_tp(tokens)
    tail = lax.all_gather(before, "tp", axis=0, tiled=False)

    filt = lax.all_to_all(filters.reshape(CTX, 1, -1), "ctx", 0, 0, tiled=True)
    table = toeplitz(filt.reshape(128, 128).astype(F32))

    mixed, blocks = project(
        pieces,
        tail,
        kv_mine,
        kv_other,
        taps[1:],
        [
            jax.ShapeDtypeStruct((rows, chan), BF16),
            jax.ShapeDtypeStruct((CTX, 32, 256), BF16),
        ],
    )
    sent = lax.all_to_all(blocks, "ctx", 0, 0, tiled=True)

    q_mine, q_other = gather_weights(w_in[0])
    (query,) = project(
        pieces, tail, q_mine, q_other, taps[:1], [jax.ShapeDtypeStruct((rows, chan), F32)]
    )

    result = conv(sent.reshape(CTX * 32, 256), table)
    back = lax.all_to_all(result.reshape(CTX, 32, 256), "ctx", 0, 0, tiled=True)
    gated = gate(back, mixed, query, skip[None, :])

    route = []
    for z in range(NZ):
        for r in range(4):
            for j in range(TP):
                route.append(((4 * z + r) * TP + j, (4 * j + r) * TP + z))
    turned = lax.ppermute(w_out, ("ctx", "tp"), route)
    o_mine, o_other = gather_weights(turned)
    return output(gather_tp(gated), o_mine, o_other)


def solution(mesh):
    return jax.shard_map(
        local,
        mesh=mesh,
        in_specs=(
            P("ctx", "tp"),
            P(None, "ctx", "tp"),
            P(None, "tp", None),
            P("tp", "ctx"),
            P("tp"),
            P("tp", "ctx"),
        ),
        out_specs=P("ctx", "tp"),
        check_vma=False,
    )
```

```python
import functools

import jax
import jax.numpy as jnp
from jax import lax
from jax.experimental import pallas as pl
from jax.experimental.pallas import tpu as pltpu
from jax.sharding import PartitionSpec as P

F32 = jnp.float32
BF16 = jnp.bfloat16
HBM = pl.BlockSpec(memory_space=pltpu.HBM)
VMEM = pl.BlockSpec(memory_space=pltpu.VMEM)
MIB = 1024 * 1024

NZ, NX = 8, 4
CTX = NZ * 4
TP = NX * 2
TAIL = 16


def barrier(*arrays):
    return lax.optimization_barrier(arrays)


def shift_z(block, step):
    route = [(i, (i + 4 * step) % CTX) for i in range(CTX)]
    return lax.ppermute(block, "ctx", route)


def swap_ctx(block, mask):
    return lax.ppermute(block, "ctx", [(i, i ^ mask) for i in range(CTX)])


def swap_core(block):
    return swap_ctx(block, 1)


def swap_ylo(block):
    return swap_ctx(block, 2)


def shift_x(block, step):
    route = [(j, (j + 2 * step) % TP) for j in range(TP)]
    return lax.ppermute(block, "tp", route)


def swap_yhi(block):
    return lax.ppermute(block, "tp", [(j, j ^ 1) for j in range(TP)])


def gather_z(block):
    groups = [[4 * z + rest for z in range(NZ)] for rest in range(4)]
    return lax.all_gather(block, "ctx", axis=0, tiled=False, axis_index_groups=groups)


def gather_tp(own):
    half = own.shape[0] // 2
    near = swap_yhi(own)
    own_right, own_left = shift_x(own, 1), shift_x(own, -1)
    near_right, near_left = shift_x(near, 1), shift_x(near, -1)
    far_right = shift_x(jnp.concatenate([own_right[:half], near_right[:half]]), 1)
    far_left = shift_x(jnp.concatenate([own_left[half:], near_left[half:]]), -1)
    return [own, near, own_right, own_left, near_right, near_left, far_right, far_left]


def piece_copies(pieces, dst, first_row, sem):
    me = lax.axis_index("tp")
    x, y = me // 2, me % 2
    width = pieces[0].shape[1]
    rows = pieces[0].shape[0]
    half = rows // 2

    def place(dx, dy, begin, count):
        there = ((x + dx + NX) % NX) * 2 + (y + dy) % 2
        lanes = pl.ds(pl.multiple_of(there * width, width), width)
        return dst.at[pl.ds(first_row + begin, count), lanes]

    whole = [(0, 0), (0, 1), (-1, 0), (1, 0), (-1, 1), (1, 1)]
    copies = []
    for ref, (dx, dy) in zip(pieces[:6], whole):
        copies.append((ref, place(dx, dy, 0, rows)))
    for ref, begin in ((pieces[6], 0), (pieces[7], half)):
        for dy in (0, 1):
            copies.append((ref.at[pl.ds(dy * half, half)], place(2, dy, begin, half)))
    return [pltpu.make_async_copy(src, to, sem) for src, to in copies]


def weight_slots():
    me = lax.axis_index("ctx")
    return me // 4, (me // 2) % 2, me % 2


def weight_copies(weights, wts, lanes):
    z, y, core = weight_slots()
    copies = []
    for dc, ref in enumerate(weights):
        for dy in (0, 1):
            slot = ((y + dy) % 2) * 2 + (core + dc) % 2
            src = ref.at[:, dy, pl.ds(0, wts.shape[2]), lanes]
            copies.append((src, wts.at[:, slot, :, lanes]))
    return copies


def pack_kernel(moves, *refs):
    *sources, out, sem = refs
    copies = [
        pltpu.make_async_copy(sources[k].at[src], out.at[dst], sem) for k, src, dst in moves
    ]
    for copy in copies:
        copy.start()
    for copy in copies:
        copy.wait()


def pack(sources, shape, moves, name):
    return pl.pallas_call(
        functools.partial(pack_kernel, moves),
        out_shape=jax.ShapeDtypeStruct(shape, sources[0].dtype),
        in_specs=[HBM] * len(sources),
        out_specs=VMEM,
        scratch_shapes=[pltpu.SemaphoreType.DMA],
        compiler_params=pltpu.CompilerParams(vmem_limit_bytes=8 * MIB),
        name=name,
    )(*sources)


def last_rows(pieces):
    rows, width = pieces[0].shape
    half = rows // 2
    moves = [(k, (pl.ds(rows - TAIL, TAIL),), (k,)) for k in range(6)]
    moves.append((6, (pl.ds(half - TAIL, TAIL),), (6,)))
    moves.append((6, (pl.ds(rows - TAIL, TAIL),), (7,)))
    return pack([*pieces[:6], pieces[7]], (TP, TAIL, width), moves, "tail")


def tail_places(tail, dst):
    me = lax.axis_index("tp")
    x, y = me // 2, me % 2
    width = tail.shape[2]
    offsets = [(0, 0), (0, 1), (-1, 0), (1, 0), (-1, 1), (1, 1), (2, 0), (2, 1)]
    places = []
    for k, (dx, dy) in enumerate(offsets):
        there = ((x + dx + NX) % NX) * 2 + (y + dy) % 2
        lanes = pl.ds(pl.multiple_of(there * width, width), width)
        places.append((tail.at[k], dst.at[pl.ds(0, TAIL), lanes]))
    return places


def project_kernel(n_proj, n_out, width, *refs):
    pieces = refs[:8]
    tail, *weights, taps = refs[8:-6 - n_out]
    outs = refs[-6 - n_out : -6]
    tok, wts, part, tok_sem, tail_sem, w_sems = refs[-6:]
    rows = pieces[0].shape[0]
    total = wts.shape[3]
    chan = total // n_proj
    n_tiles = chan // width
    copies = piece_copies(pieces, tok, TAIL, tok_sem)
    for ref, to in tail_places(tail, tok):
        copies.append(pltpu.make_async_copy(ref, to, tail_sem))
    for copy in copies:
        copy.start()
    w_copies = []
    for tile in range(n_tiles):
        group = []
        for proj in range(n_proj):
            lanes = pl.ds(proj * chan + tile * width, width)
            for src, to in weight_copies(weights, wts, lanes):
                group.append(pltpu.make_async_copy(src, to, w_sems.at[tile]))
        for copy in group:
            copy.start()
        w_copies.append(group)
    for copy in copies:
        copy.wait()
    for tile in range(n_tiles):
        for copy in w_copies[tile]:
            copy.wait()
        smooth = []
        for proj in range(n_proj):
            lanes = pl.ds(proj * chan + tile * width, width)
            weights = wts[:, :, :, lanes].reshape(-1, width)
            product = jnp.dot(tok[...], weights, preferred_element_type=F32)
            part[proj] = product.astype(BF16).astype(F32)
            cols = pl.ds(tile * width, width)
            value = taps[proj, 0:1, cols] * part[proj, pl.ds(TAIL, rows), :]
            value = value + taps[proj, 1:2, cols] * part[proj, pl.ds(TAIL - 1, rows), :]
            value = value + taps[proj, 2:3, cols] * part[proj, pl.ds(TAIL - 2, rows), :]
            smooth.append(value)
        cols = pl.ds(tile * width, width)
        if n_proj == 1:
            outs[0][:, cols] = smooth[0]
        else:
            mixed = smooth[0] * smooth[1]
            outs[0][:, cols] = mixed.astype(BF16)
            turned = mixed.T.astype(BF16)
            for a in range(2):
                block = turned[:, 256 * a : 256 * a + 256].reshape(width // 16, 16, 256)
                outs[1][pl.ds(tile * (width // 16), width // 16), pl.ds(16 * a, 16), :] = block


def project(pieces, tail, weights, taps, out_shapes):
    n_proj = taps.shape[0]
    total = weights[0].shape[-1]
    width = 256
    n_tiles = total // n_proj // width
    rows = pieces[0].shape[0]
    depth = TP * pieces[0].shape[1]
    return pl.pallas_call(
        functools.partial(project_kernel, n_proj, len(out_shapes), width),
        out_shape=out_shapes,
        in_specs=[HBM] * (9 + len(weights)) + [VMEM],
        out_specs=[VMEM] * len(out_shapes),
        scratch_shapes=[
            pltpu.VMEM((TAIL + rows, depth), BF16),
            pltpu.VMEM((NZ, 4, depth // CTX, total), BF16),
            pltpu.VMEM((n_proj, TAIL + rows, width), F32),
            pltpu.SemaphoreType.DMA,
            pltpu.SemaphoreType.DMA,
            pltpu.SemaphoreType.DMA((n_tiles,)),
        ],
        compiler_params=pltpu.CompilerParams(vmem_limit_bytes=60 * MIB),
        name="project%d" % n_proj,
    )(*pieces, tail, *weights, taps)


def toeplitz_kernel(mine, other, out_hbm, out_ref, rows_ref, seg_ref, row_sem, sem):
    _, y, core = weight_slots()
    group = lax.axis_index("ctx")
    width = rows_ref.shape[3]
    lanes = pl.ds(pl.multiple_of(group // 16 * width, width), width)
    filter_rows = pl.ds(mine.shape[2] - 16, 16)
    copies = []
    for dc, ref in enumerate((mine, other)):
        for dy in (0, 1):
            slot = ((y + dy) % 2) * 2 + (core + dc) % 2
            src = ref.at[:, dy, filter_rows, lanes]
            copies.append(pltpu.make_async_copy(src, rows_ref.at[:, slot], row_sem))
    for copy in copies:
        copy.start()
    for copy in copies:
        copy.wait()
    chosen = lax.broadcasted_iota(jnp.int32, (16, width), 0) == group % 16
    for k in range(CTX):
        block = rows_ref[k // 4, k % 4].astype(F32)
        row = jnp.sum(jnp.where(chosen, block, 0.0), axis=0, keepdims=True)
        for q in range(4):
            seg_ref[4 * k + q : 4 * k + q + 1, :] = row[:, 128 * q : 128 * q + 128]
    low = lax.broadcasted_iota(jnp.int32, (128, 128), 1) >= lax.broadcasted_iota(
        jnp.int32, (128, 128), 0
    )

    def turn(m):
        row = jnp.broadcast_to(seg_ref[pl.ds(m, 1), :], (128, 128))
        return pltpu.roll(row, 0, 1, stride=1, stride_axis=0)

    def body(d, before):
        even = turn(2 * d)
        odd = turn(2 * d + 1)
        same = jnp.where(low, even, before).astype(BF16)
        second = jnp.where(low, odd, even).astype(BF16)
        out_ref[d, 0:128, 0:128] = same
        out_ref[d, 128:256, 128:256] = same
        out_ref[d, 0:128, 128:256] = second
        out_ref[d + 1, 128:256, 0:128] = second
        return odd

    def copy_out(g):
        here = pl.ds(g * 8, 8)
        return pltpu.make_async_copy(out_ref.at[here], out_hbm.at[here], sem.at[g])

    out_ref[0, 128:256, 0:128] = jnp.zeros((128, 128), BF16)
    before = jnp.zeros((128, 128), F32)
    for g in range(8):
        before = lax.fori_loop(g * 8, g * 8 + 8, body, before)
        copy_out(g).start()
    for g in range(8):
        copy_out(g).wait()


def toeplitz(weights):
    return pl.pallas_call(
        toeplitz_kernel,
        out_shape=jax.ShapeDtypeStruct((64, 256, 256), BF16),
        in_specs=[HBM] * 2,
        out_specs=HBM,
        scratch_shapes=[
            pltpu.VMEM((65, 256, 256), BF16),
            pltpu.VMEM((NZ, 4, 16, 512), BF16),
            pltpu.VMEM((128, 128), F32),
            pltpu.SemaphoreType.DMA,
            pltpu.SemaphoreType.DMA((8,)),
        ],
        compiler_params=pltpu.CompilerParams(vmem_limit_bytes=60 * MIB),
        name="toeplitz",
    )(*weights)


FOLD = 4


def conv_kernel(x_ref, h_hbm, y_ref, wide, acc, h_ref, sems):
    rows = x_ref.shape[0]
    steps = h_ref.shape[0]
    copies = [pltpu.make_async_copy(h_hbm.at[g], h_ref.at[g], sems.at[g]) for g in range(steps)]
    for copy in copies:
        copy.start()
    for k in range(FOLD):
        if k:
            wide[0 : 16 * k, 256 * k : 256 * k + 256] = jnp.zeros((16 * k, 256), BF16)
        wide[16 * k : rows, 256 * k : 256 * k + 256] = x_ref[0 : rows - 16 * k, :]
    for g in range(steps):
        copies[g].wait()
        skip = 16 * FOLD * g
        product = jnp.dot(wide[0 : rows - skip, :], h_ref[g], preferred_element_type=F32)
        if g == 0:
            acc[...] = product
        else:
            acc[skip:rows, :] += product
    y_ref[...] = acc[...].astype(BF16)


def conv(x, table):
    rows = x.shape[0]
    steps = 64 // FOLD
    return pl.pallas_call(
        conv_kernel,
        out_shape=jax.ShapeDtypeStruct((rows, 256), BF16),
        in_specs=[VMEM, HBM],
        out_specs=VMEM,
        scratch_shapes=[
            pltpu.VMEM((rows, FOLD * 256), BF16),
            pltpu.VMEM((rows, 256), F32),
            pltpu.VMEM((steps, FOLD * 256, 256), BF16),
            pltpu.SemaphoreType.DMA((steps,)),
        ],
        compiler_params=pltpu.CompilerParams(vmem_limit_bytes=60 * MIB),
        name="conv",
    )(x, table.reshape(steps, FOLD * 256, 256))


def gate_kernel(back_ref, mixed_ref, query_ref, skip_ref, out_ref):
    chan = mixed_ref.shape[1]
    for a in range(2):
        block = back_ref[:, 16 * a : 16 * a + 16, :].reshape(chan, 256)
        turned = block.astype(F32).T
        here = pl.ds(256 * a, 256)
        mixed = mixed_ref[here, :].astype(F32)
        out_ref[here, :] = (query_ref[here, :] * (turned + skip_ref[...] * mixed)).astype(BF16)


def gate(back, mixed, query, skip):
    return pl.pallas_call(
        gate_kernel,
        out_shape=jax.ShapeDtypeStruct(mixed.shape, BF16),
        in_specs=[VMEM] * 4,
        out_specs=VMEM,
        compiler_params=pltpu.CompilerParams(vmem_limit_bytes=8 * MIB),
        name="gate",
    )(back, mixed, query, skip)


def output_kernel(*refs):
    pieces = refs[:8]
    mine, other, out_ref, act, wts, act_sem, w_sem = refs[8:]
    z, y, core = weight_slots()
    copies = piece_copies(pieces, act, 0, act_sem)
    depth, width = mine.shape[2:]
    for ref, dc in ((mine, 0), (other, 1)):
        for dy in (0, 1):
            slot = ((y + dy) % 2) * 2 + (core + dc) % 2
            lanes = pl.ds(pl.multiple_of(slot * width, width), width)
            copies.append(pltpu.make_async_copy(ref.at[:, dy], wts.at[:, :, lanes], w_sem))
    for copy in copies:
        copy.start()
    for copy in copies:
        copy.wait()
    weights = wts[...].reshape(-1, wts.shape[2])
    out_ref[...] = jnp.dot(act[...], weights, preferred_element_type=F32).astype(BF16)


def output(pieces, mine, other):
    rows, part = pieces[0].shape
    depth, width = mine.shape[2:]
    return pl.pallas_call(
        output_kernel,
        out_shape=jax.ShapeDtypeStruct((rows, 4 * width), BF16),
        in_specs=[HBM] * 10,
        out_specs=VMEM,
        scratch_shapes=[
            pltpu.VMEM((rows, TP * part), BF16),
            pltpu.VMEM((NZ, depth, 4 * width), BF16),
            pltpu.SemaphoreType.DMA,
            pltpu.SemaphoreType.DMA,
        ],
        compiler_params=pltpu.CompilerParams(vmem_limit_bytes=60 * MIB),
        name="output",
    )(*pieces, mine, other)


def pair_ylo(own):
    return jnp.stack([own, swap_ylo(own)])


def local(tokens, w_in, short_taps, filters, skip, w_out):
    rows, _ = tokens.shape
    depth, chan = w_in.shape[1:]
    taps = short_taps.transpose(0, 2, 1)

    kv = jnp.concatenate([w_in[1], w_in[2]], axis=1)
    filt = jnp.concatenate([filters[:16], filters[16:]], axis=1)
    kv_mine = gather_z(pair_ylo(jnp.concatenate([kv, filt])))
    pieces = gather_tp(tokens)
    tail = last_rows(pieces)
    tail = lax.ppermute(tail, "ctx", [(i, i + 1) for i in range(CTX - 1)])

    kv_mine, tail, *pieces = barrier(kv_mine, tail, *pieces)
    w_in, w_out, kv_mine = barrier(w_in, w_out, kv_mine)
    kv_other = swap_core(kv_mine)
    q_pair = pair_ylo(w_in[0])
    route = []
    for z in range(NZ):
        for r in range(4):
            for j in range(TP):
                route.append(((4 * z + r) * TP + j, (4 * j + r) * TP + z))
    w_out = lax.ppermute(w_out, ("ctx", "tp"), route)
    mixed, blocks = project(
        pieces,
        tail,
        (kv_mine, kv_other),
        taps[1:],
        [
            jax.ShapeDtypeStruct((rows, chan), BF16),
            jax.ShapeDtypeStruct((CTX, 32, 256), BF16),
        ],
    )

    q_pair, w_out, blocks = barrier(q_pair, w_out, blocks)
    q_mine = gather_z(q_pair)
    o_pair = pair_ylo(w_out)
    sent = lax.all_to_all(blocks, "ctx", 0, 0, tiled=True)
    table = toeplitz((kv_mine, kv_other))
    o_pair, sent, table = barrier(o_pair, sent, table)
    result = conv(sent.reshape(CTX * 32, 256), table)
    q_mine, result = barrier(q_mine, result)
    back = lax.all_to_all(result.reshape(CTX, 32, 256), "ctx", 0, 0, tiled=True)
    (query,) = project(
        pieces,
        tail,
        (q_mine, swap_core(q_mine)),
        taps[:1],
        [jax.ShapeDtypeStruct((rows, chan), F32)],
    )
    gated = gate(back, mixed, query, skip[None, :])

    o_pair, q_mine = barrier(o_pair, q_mine)
    o_mine = gather_z(o_pair)
    o_mine, *gathered = barrier(o_mine, *gather_tp(gated))
    return output(gathered, o_mine, swap_core(o_mine))


def solution(mesh):
    return jax.shard_map(
        local,
        mesh=mesh,
        in_specs=(
            P("ctx", "tp"),
            P(None, "ctx", "tp"),
            P(None, "tp", None),
            P("tp", "ctx"),
            P("tp"),
            P("tp", "ctx"),
        ),
        out_specs=P("ctx", "tp"),
        check_vma=False,
    )
```

```python
import functools

import jax
import jax.numpy as jnp
from jax import lax
from jax.experimental import pallas as pl
from jax.experimental.pallas import tpu as pltpu
from jax.sharding import PartitionSpec as P

F32 = jnp.float32
BF16 = jnp.bfloat16
HBM = pl.BlockSpec(memory_space=pltpu.HBM)
VMEM = pl.BlockSpec(memory_space=pltpu.VMEM)
MIB = 1024 * 1024

NZ, NX = 8, 4
CTX = NZ * 4
TP = NX * 2
TAIL = 16


def barrier(*arrays):
    return lax.optimization_barrier(arrays)


def shift_z(block, step):
    route = [(i, (i + 4 * step) % CTX) for i in range(CTX)]
    return lax.ppermute(block, "ctx", route)


def swap_ctx(block, mask):
    return lax.ppermute(block, "ctx", [(i, i ^ mask) for i in range(CTX)])


def swap_core(block):
    return swap_ctx(block, 1)


def swap_ylo(block):
    return swap_ctx(block, 2)


def shift_x(block, step):
    route = [(j, (j + 2 * step) % TP) for j in range(TP)]
    return lax.ppermute(block, "tp", route)


def swap_yhi(block):
    return lax.ppermute(block, "tp", [(j, j ^ 1) for j in range(TP)])


def gather_z(block):
    groups = [[4 * z + rest for z in range(NZ)] for rest in range(4)]
    return lax.all_gather(block, "ctx", axis=0, tiled=False, axis_index_groups=groups)


def gather_tp(own, first=None):
    half = own.shape[0] // 2
    near = swap_yhi(own)
    if first is not None:
        near, first = barrier(near, first)
    own_right, own_left = shift_x(own, 1), shift_x(own, -1)
    near_right, near_left = shift_x(near, 1), shift_x(near, -1)
    far_right = shift_x(jnp.concatenate([own_right[:half], near_right[:half]]), 1)
    far_left = shift_x(jnp.concatenate([own_left[half:], near_left[half:]]), -1)
    pieces = [own, near, own_right, own_left, near_right, near_left, far_right, far_left]
    return pieces, first


def piece_copies(pieces, dst, first_row, sem):
    me = lax.axis_index("tp")
    x, y = me // 2, me % 2
    width = pieces[0].shape[1]
    rows = pieces[0].shape[0]
    half = rows // 2

    def place(dx, dy, begin, count):
        there = ((x + dx + NX) % NX) * 2 + (y + dy) % 2
        lanes = pl.ds(pl.multiple_of(there * width, width), width)
        return dst.at[pl.ds(first_row + begin, count), lanes]

    whole = [(0, 0), (0, 1), (-1, 0), (1, 0), (-1, 1), (1, 1)]
    copies = []
    for ref, (dx, dy) in zip(pieces[:6], whole):
        copies.append((ref, place(dx, dy, 0, rows)))
    for ref, begin in ((pieces[6], 0), (pieces[7], half)):
        for dy in (0, 1):
            copies.append((ref.at[pl.ds(dy * half, half)], place(2, dy, begin, half)))
    return [pltpu.make_async_copy(src, to, sem) for src, to in copies]


def weight_slots():
    me = lax.axis_index("ctx")
    return me // 4, (me // 2) % 2, me % 2


def weight_copies(weights, wts, lanes):
    z, y, core = weight_slots()
    copies = []
    for dc, ref in enumerate(weights):
        for dy in (0, 1):
            slot = ((y + dy) % 2) * 2 + (core + dc) % 2
            src = ref.at[:, dy, pl.ds(0, wts.shape[2]), lanes]
            copies.append((src, wts.at[:, slot, :, lanes]))
    return copies


def pack_kernel(moves, *refs):
    *sources, out, sem = refs
    copies = [
        pltpu.make_async_copy(sources[k].at[src], out.at[dst], sem) for k, src, dst in moves
    ]
    for copy in copies:
        copy.start()
    for copy in copies:
        copy.wait()


def pack(sources, shape, moves, name):
    return pl.pallas_call(
        functools.partial(pack_kernel, moves),
        out_shape=jax.ShapeDtypeStruct(shape, sources[0].dtype),
        in_specs=[HBM] * len(sources),
        out_specs=VMEM,
        scratch_shapes=[pltpu.SemaphoreType.DMA],
        compiler_params=pltpu.CompilerParams(vmem_limit_bytes=8 * MIB),
        name=name,
    )(*sources)


def last_rows(pieces):
    rows, width = pieces[0].shape
    half = rows // 2
    moves = [(k, (pl.ds(rows - TAIL, TAIL),), (k,)) for k in range(6)]
    moves.append((6, (pl.ds(half - TAIL, TAIL),), (6,)))
    moves.append((6, (pl.ds(rows - TAIL, TAIL),), (7,)))
    return pack([*pieces[:6], pieces[7]], (TP, TAIL, width), moves, "tail")


def tail_places(tail, dst):
    me = lax.axis_index("tp")
    x, y = me // 2, me % 2
    width = tail.shape[2]
    offsets = [(0, 0), (0, 1), (-1, 0), (1, 0), (-1, 1), (1, 1), (2, 0), (2, 1)]
    places = []
    for k, (dx, dy) in enumerate(offsets):
        there = ((x + dx + NX) % NX) * 2 + (y + dy) % 2
        lanes = pl.ds(pl.multiple_of(there * width, width), width)
        places.append((tail.at[k], dst.at[pl.ds(0, TAIL), lanes]))
    return places


def project_kernel(n_proj, n_out, width, *refs):
    pieces = refs[:8]
    tail, *weights, taps = refs[8:-6 - n_out]
    outs = refs[-6 - n_out : -6]
    tok, wts, part, tok_sem, tail_sem, w_sems = refs[-6:]
    rows = pieces[0].shape[0]
    total = wts.shape[3]
    chan = total // n_proj
    n_tiles = chan // width
    copies = piece_copies(pieces, tok, TAIL, tok_sem)
    for ref, to in tail_places(tail, tok):
        copies.append(pltpu.make_async_copy(ref, to, tail_sem))
    for copy in copies:
        copy.start()
    w_copies = []
    for tile in range(n_tiles):
        group = []
        for proj in range(n_proj):
            lanes = pl.ds(proj * chan + tile * width, width)
            for src, to in weight_copies(weights, wts, lanes):
                group.append(pltpu.make_async_copy(src, to, w_sems.at[tile]))
        for copy in group:
            copy.start()
        w_copies.append(group)
    for copy in copies:
        copy.wait()
    for tile in range(n_tiles):
        for copy in w_copies[tile]:
            copy.wait()
        smooth = []
        for proj in range(n_proj):
            lanes = pl.ds(proj * chan + tile * width, width)
            weights = wts[:, :, :, lanes].reshape(-1, width)
            product = jnp.dot(tok[...], weights, preferred_element_type=F32)
            part[proj] = product.astype(BF16).astype(F32)
            cols = pl.ds(tile * width, width)
            value = taps[proj, 0:1, cols] * part[proj, pl.ds(TAIL, rows), :]
            value = value + taps[proj, 1:2, cols] * part[proj, pl.ds(TAIL - 1, rows), :]
            value = value + taps[proj, 2:3, cols] * part[proj, pl.ds(TAIL - 2, rows), :]
            smooth.append(value)
        cols = pl.ds(tile * width, width)
        if n_proj == 1:
            outs[0][:, cols] = smooth[0]
        else:
            mixed = smooth[0] * smooth[1]
            outs[0][:, cols] = mixed.astype(BF16)
            turned = mixed.T.astype(BF16)
            for a in range(2):
                block = turned[:, 256 * a : 256 * a + 256].reshape(width // 16, 16, 256)
                outs[1][pl.ds(tile * (width // 16), width // 16), pl.ds(16 * a, 16), :] = block


def project(pieces, tail, weights, taps, out_shapes):
    n_proj = taps.shape[0]
    total = weights[0].shape[-1]
    width = 256
    n_tiles = total // n_proj // width
    rows = pieces[0].shape[0]
    depth = TP * pieces[0].shape[1]
    return pl.pallas_call(
        functools.partial(project_kernel, n_proj, len(out_shapes), width),
        out_shape=out_shapes,
        in_specs=[HBM] * (9 + len(weights)) + [VMEM],
        out_specs=[VMEM] * len(out_shapes),
        scratch_shapes=[
            pltpu.VMEM((TAIL + rows, depth), BF16),
            pltpu.VMEM((NZ, 4, depth // CTX, total), BF16),
            pltpu.VMEM((n_proj, TAIL + rows, width), F32),
            pltpu.SemaphoreType.DMA,
            pltpu.SemaphoreType.DMA,
            pltpu.SemaphoreType.DMA((n_tiles,)),
        ],
        compiler_params=pltpu.CompilerParams(vmem_limit_bytes=60 * MIB),
        name="project%d" % n_proj,
    )(*pieces, tail, *weights, taps)


def toeplitz_kernel(mine, other, out_hbm, out_ref, rows_ref, seg_ref, row_sem, sem):
    _, y, core = weight_slots()
    group = lax.axis_index("ctx")
    width = rows_ref.shape[3]
    lanes = pl.ds(pl.multiple_of(group // 16 * width, width), width)
    filter_rows = pl.ds(mine.shape[2] - 16, 16)
    copies = []
    for dc, ref in enumerate((mine, other)):
        for dy in (0, 1):
            slot = ((y + dy) % 2) * 2 + (core + dc) % 2
            src = ref.at[:, dy, filter_rows, lanes]
            copies.append(pltpu.make_async_copy(src, rows_ref.at[:, slot], row_sem))
    for copy in copies:
        copy.start()
    for copy in copies:
        copy.wait()
    chosen = lax.broadcasted_iota(jnp.int32, (16, width), 0) == group % 16
    for k in range(CTX):
        block = rows_ref[k // 4, k % 4].astype(F32)
        row = jnp.sum(jnp.where(chosen, block, 0.0), axis=0, keepdims=True)
        for q in range(4):
            seg_ref[4 * k + q : 4 * k + q + 1, :] = row[:, 128 * q : 128 * q + 128]
    low = lax.broadcasted_iota(jnp.int32, (128, 128), 1) >= lax.broadcasted_iota(
        jnp.int32, (128, 128), 0
    )

    def turn(m):
        row = jnp.broadcast_to(seg_ref[pl.ds(m, 1), :], (128, 128))
        return pltpu.roll(row, 0, 1, stride=1, stride_axis=0)

    def body(d, before):
        even = turn(2 * d)
        odd = turn(2 * d + 1)
        same = jnp.where(low, even, before).astype(BF16)
        second = jnp.where(low, odd, even).astype(BF16)
        out_ref[d, 0:128, 0:128] = same
        out_ref[d, 128:256, 128:256] = same
        out_ref[d, 0:128, 128:256] = second
        out_ref[d + 1, 128:256, 0:128] = second
        return odd

    def copy_out(g):
        here = pl.ds(g * 8, 8)
        return pltpu.make_async_copy(out_ref.at[here], out_hbm.at[here], sem.at[g])

    out_ref[0, 128:256, 0:128] = jnp.zeros((128, 128), BF16)
    before = jnp.zeros((128, 128), F32)
    for g in range(8):
        before = lax.fori_loop(g * 8, g * 8 + 8, body, before)
        copy_out(g).start()
    for g in range(8):
        copy_out(g).wait()


def toeplitz(weights):
    return pl.pallas_call(
        toeplitz_kernel,
        out_shape=jax.ShapeDtypeStruct((64, 256, 256), BF16),
        in_specs=[HBM] * 2,
        out_specs=HBM,
        scratch_shapes=[
            pltpu.VMEM((65, 256, 256), BF16),
            pltpu.VMEM((NZ, 4, 16, 512), BF16),
            pltpu.VMEM((128, 128), F32),
            pltpu.SemaphoreType.DMA,
            pltpu.SemaphoreType.DMA((8,)),
        ],
        compiler_params=pltpu.CompilerParams(vmem_limit_bytes=60 * MIB),
        name="toeplitz",
    )(*weights)


TILE = 128
LAGS = TILE // 16
FETCHES = 4


def conv_kernel(x_ref, h_hbm, y_ref, h_ref, sems):
    rows, width = x_ref.shape
    tiles = rows // TILE

    def fetch(g):
        count = h_ref.shape[0] // FETCHES
        here = pl.ds(g * count, count)
        return pltpu.make_async_copy(h_hbm.at[here], h_ref.at[here], sems.at[g])

    for g in range(FETCHES):
        fetch(g).start()
    for tile in range(tiles):
        if tile % (tiles // FETCHES) == 0:
            fetch(tile // (tiles // FETCHES)).wait()
        lags = (tile + 1) * LAGS
        shifted = []
        for lag in range(lags):
            first = tile * TILE - 16 * lag
            if first >= 0:
                shifted.append(x_ref[first : first + TILE, :])
            else:
                empty = jnp.zeros((-first, width), BF16)
                shifted.append(jnp.concatenate([empty, x_ref[0 : TILE + first, :]], axis=0))
        product = jnp.dot(
            jnp.concatenate(shifted, axis=1),
            h_ref[0 : lags * width, :],
            preferred_element_type=F32,
        )
        y_ref[tile * TILE : tile * TILE + TILE, :] = product.astype(BF16)


def conv(x, table):
    rows, width = x.shape
    return pl.pallas_call(
        conv_kernel,
        out_shape=jax.ShapeDtypeStruct((rows, width), BF16),
        in_specs=[VMEM, HBM],
        out_specs=VMEM,
        scratch_shapes=[
            pltpu.VMEM((64 * width, width), BF16),
            pltpu.SemaphoreType.DMA((FETCHES,)),
        ],
        compiler_params=pltpu.CompilerParams(vmem_limit_bytes=60 * MIB),
        name="conv",
    )(x, table.reshape(64 * width, width))


def gate_kernel(back_ref, mixed_ref, query_ref, skip_ref, out_ref):
    chan = mixed_ref.shape[1]
    for a in range(2):
        block = back_ref[:, 16 * a : 16 * a + 16, :].reshape(chan, 256)
        turned = block.astype(F32).T
        here = pl.ds(256 * a, 256)
        mixed = mixed_ref[here, :].astype(F32)
        out_ref[here, :] = (query_ref[here, :] * (turned + skip_ref[...] * mixed)).astype(BF16)


def gate(back, mixed, query, skip):
    return pl.pallas_call(
        gate_kernel,
        out_shape=jax.ShapeDtypeStruct(mixed.shape, BF16),
        in_specs=[VMEM] * 4,
        out_specs=VMEM,
        compiler_params=pltpu.CompilerParams(vmem_limit_bytes=8 * MIB),
        name="gate",
    )(back, mixed, query, skip)


def near_parts(pieces):
    me = lax.axis_index("tp")
    x, y = me // 2, me % 2
    offsets = [(0, 0), (0, 1), (-1, 0), (1, 0), (-1, 1), (1, 1)]
    parts = []
    for ref, (dx, dy) in zip(pieces, offsets):
        parts.append((((x + dx + NX) % NX) * 2 + (y + dy) % 2, [(ref, 0)]))
    return parts


def far_parts(pieces):
    me = lax.axis_index("tp")
    x, y = me // 2, me % 2
    half = pieces[0].shape[0] // 2
    parts = []
    for dy in (0, 1):
        rows = pl.ds(dy * half, half)
        there = ((x + 2) % NX) * 2 + (y + dy) % 2
        parts.append((there, [(pieces[0].at[rows], 0), (pieces[1].at[rows], half)]))
    return parts


def output_kernel(parts_of, n_pieces, *refs):
    pieces, (weights, *start) = refs[:n_pieces], refs[n_pieces:-4]
    out_ref, act, wts, sem = refs[-4:]
    _, y, core = weight_slots()
    width = weights.shape[3]
    depth = wts.shape[1]
    copies = []
    for p, (there, sources) in enumerate(parts_of(pieces)):
        for src, first in sources:
            to = act.at[pl.ds(first, src.shape[0]), pl.ds(p * depth, depth)]
            copies.append(pltpu.make_async_copy(src, to, sem))
        for k in range(4):
            slot = ((y + k // 2) % 2) * 2 + (core + k % 2) % 2
            lanes = pl.ds(pl.multiple_of(slot * width, width), width)
            to = wts.at[p, :, lanes]
            copies.append(pltpu.make_async_copy(weights.at[there, k], to, sem))
    for copy in copies:
        copy.start()
    for copy in copies:
        copy.wait()
    matrix = wts[...].reshape(-1, wts.shape[2])
    total = jnp.dot(act[...], matrix, preferred_element_type=F32)
    if start:
        total = total + start[0][...]
    out_ref[...] = total.astype(out_ref.dtype)


def output(pieces, parts_of, parts, weights, start, dtype):
    rows = pieces[0].shape[0]
    depth, width = weights.shape[2:]
    return pl.pallas_call(
        functools.partial(output_kernel, parts_of, len(pieces)),
        out_shape=jax.ShapeDtypeStruct((rows, 4 * width), dtype),
        in_specs=[HBM] * (len(pieces) + 1) + [VMEM] * len(start),
        out_specs=VMEM,
        scratch_shapes=[
            pltpu.VMEM((rows, parts * depth), BF16),
            pltpu.VMEM((parts, depth, 4 * width), BF16),
            pltpu.SemaphoreType.DMA,
        ],
        compiler_params=pltpu.CompilerParams(vmem_limit_bytes=60 * MIB),
        name="output%d" % parts,
    )(*pieces, weights, *start)


def pair_ylo(own):
    return jnp.stack([own, swap_ylo(own)])


def local(tokens, w_in, short_taps, filters, skip, w_out):
    rows, _ = tokens.shape
    depth, chan = w_in.shape[1:]
    taps = short_taps.transpose(0, 2, 1)

    kv = jnp.concatenate([w_in[1], w_in[2]], axis=1)
    filt = jnp.concatenate([filters[:16], filters[16:]], axis=1)
    kv_mine = gather_z(pair_ylo(jnp.concatenate([kv, filt])))
    route = []
    for z in range(NZ):
        for r in range(4):
            for j in range(TP):
                route.append(((4 * z + r) * TP + j, (4 * j + r) * TP + z))
    w_out = lax.ppermute(w_out, ("ctx", "tp"), route)
    pieces, w_out = gather_tp(tokens, w_out)
    tail = last_rows(pieces)
    tail = lax.ppermute(tail, "ctx", [(i, i + 1) for i in range(CTX - 1)])

    kv_mine, tail, *pieces = barrier(kv_mine, tail, *pieces)
    w_in, kv_mine = barrier(w_in, kv_mine)
    kv_other = swap_core(kv_mine)
    q_mine = gather_z(pair_ylo(w_in[0]))
    mixed, blocks = project(
        pieces,
        tail,
        (kv_mine, kv_other),
        taps[1:],
        [
            jax.ShapeDtypeStruct((rows, chan), BF16),
            jax.ShapeDtypeStruct((CTX, 32, 256), BF16),
        ],
    )

    w_out, blocks = barrier(w_out, blocks)
    o_pair = jnp.stack([w_out, swap_core(w_out)])
    o_pair = jnp.concatenate([o_pair, swap_ylo(o_pair)])
    sent = lax.all_to_all(blocks, "ctx", 0, 0, tiled=True)
    table = toeplitz((kv_mine, kv_other))
    o_pair, sent, table = barrier(o_pair, sent, table)
    result = conv(sent.reshape(CTX * 32, 256), table)
    q_mine, o_pair, result = barrier(q_mine, o_pair, result)
    back = lax.all_to_all(result.reshape(CTX, 32, 256), "ctx", 0, 0, tiled=True)
    o_mine = gather_z(o_pair)
    (query,) = project(
        pieces,
        tail,
        (q_mine, swap_core(q_mine)),
        taps[:1],
        [jax.ShapeDtypeStruct((rows, chan), F32)],
    )
    gated = gate(back, mixed, query, skip[None, :])

    gathered = gather_tp(gated)[0]
    total = output(gathered[:6], near_parts, 6, o_mine, [], F32)
    return output(gathered[6:], far_parts, 2, o_mine, [total], BF16)


def solution(mesh):
    return jax.shard_map(
        local,
        mesh=mesh,
        in_specs=(
            P("ctx", "tp"),
            P(None, "ctx", "tp"),
            P(None, "tp", None),
            P("tp", "ctx"),
            P("tp"),
            P("tp", "ctx"),
        ),
        out_specs=P("ctx", "tp"),
        check_vma=False,
    )
```

```python
import functools

import jax
import jax.numpy as jnp
from jax import lax
from jax.experimental import pallas as pl
from jax.experimental.pallas import tpu as pltpu
from jax.sharding import PartitionSpec as P

F32 = jnp.float32
BF16 = jnp.bfloat16
HBM = pl.BlockSpec(memory_space=pltpu.HBM)
VMEM = pl.BlockSpec(memory_space=pltpu.VMEM)
MIB = 1024 * 1024

NZ, NX = 8, 4
CTX = NZ * 4
TP = NX * 2
TAIL = 16


def barrier(*arrays):
    return lax.optimization_barrier(arrays)


def shift_z(block, step):
    route = [(i, (i + 4 * step) % CTX) for i in range(CTX)]
    return lax.ppermute(block, "ctx", route)


def swap_ctx(block, mask):
    return lax.ppermute(block, "ctx", [(i, i ^ mask) for i in range(CTX)])


def swap_core(block):
    return swap_ctx(block, 1)


def swap_ylo(block):
    return swap_ctx(block, 2)


def shift_x(block, step):
    route = [(j, (j + 2 * step) % TP) for j in range(TP)]
    return lax.ppermute(block, "tp", route)


def swap_yhi(block):
    return lax.ppermute(block, "tp", [(j, j ^ 1) for j in range(TP)])


def gather_z(block):
    groups = [[4 * z + rest for z in range(NZ)] for rest in range(4)]
    return lax.all_gather(block, "ctx", axis=0, tiled=False, axis_index_groups=groups)


def gather_tp(own, first=None):
    half = own.shape[0] // 2
    near = swap_yhi(own)
    if first is not None:
        near, first = barrier(near, first)
    own_right, own_left = shift_x(own, 1), shift_x(own, -1)
    near_right, near_left = shift_x(near, 1), shift_x(near, -1)
    far_right = shift_x(jnp.concatenate([own_right[:half], near_right[:half]]), 1)
    far_left = shift_x(jnp.concatenate([own_left[half:], near_left[half:]]), -1)
    pieces = [own, near, own_right, own_left, near_right, near_left, far_right, far_left]
    return pieces, first


def piece_copies(pieces, dst, first_row, sem):
    me = lax.axis_index("tp")
    x, y = me // 2, me % 2
    width = pieces[0].shape[1]
    rows = pieces[0].shape[0]
    half = rows // 2

    def place(dx, dy, begin, count):
        there = ((x + dx + NX) % NX) * 2 + (y + dy) % 2
        lanes = pl.ds(pl.multiple_of(there * width, width), width)
        return dst.at[pl.ds(first_row + begin, count), lanes]

    whole = [(0, 0), (0, 1), (-1, 0), (1, 0), (-1, 1), (1, 1)]
    copies = []
    for ref, (dx, dy) in zip(pieces[:6], whole):
        copies.append((ref, place(dx, dy, 0, rows)))
    for ref, begin in ((pieces[6], 0), (pieces[7], half)):
        for dy in (0, 1):
            copies.append((ref.at[pl.ds(dy * half, half)], place(2, dy, begin, half)))
    return [pltpu.make_async_copy(src, to, sem) for src, to in copies]


def weight_slots():
    me = lax.axis_index("ctx")
    return me // 4, (me // 2) % 2, me % 2


def weight_copies(weights, wts, lanes):
    z, y, core = weight_slots()
    copies = []
    for dc, ref in enumerate(weights):
        for dy in (0, 1):
            slot = ((y + dy) % 2) * 2 + (core + dc) % 2
            src = ref.at[:, dy, pl.ds(0, wts.shape[2]), lanes]
            copies.append((src, wts.at[:, slot, :, lanes]))
    return copies


def pack_kernel(moves, *refs):
    *sources, out, sem = refs
    copies = [
        pltpu.make_async_copy(sources[k].at[src], out.at[dst], sem) for k, src, dst in moves
    ]
    for copy in copies:
        copy.start()
    for copy in copies:
        copy.wait()


def pack(sources, shape, moves, name):
    return pl.pallas_call(
        functools.partial(pack_kernel, moves),
        out_shape=jax.ShapeDtypeStruct(shape, sources[0].dtype),
        in_specs=[HBM] * len(sources),
        out_specs=VMEM,
        scratch_shapes=[pltpu.SemaphoreType.DMA],
        compiler_params=pltpu.CompilerParams(vmem_limit_bytes=8 * MIB),
        name=name,
    )(*sources)


def last_rows(pieces):
    rows, width = pieces[0].shape
    half = rows // 2
    moves = [(k, (pl.ds(rows - TAIL, TAIL),), (k,)) for k in range(6)]
    moves.append((6, (pl.ds(half - TAIL, TAIL),), (6,)))
    moves.append((6, (pl.ds(rows - TAIL, TAIL),), (7,)))
    return pack([*pieces[:6], pieces[7]], (TP, TAIL, width), moves, "tail")


def tail_places(tail, dst):
    me = lax.axis_index("tp")
    x, y = me // 2, me % 2
    width = tail.shape[2]
    offsets = [(0, 0), (0, 1), (-1, 0), (1, 0), (-1, 1), (1, 1), (2, 0), (2, 1)]
    places = []
    for k, (dx, dy) in enumerate(offsets):
        there = ((x + dx + NX) % NX) * 2 + (y + dy) % 2
        lanes = pl.ds(pl.multiple_of(there * width, width), width)
        places.append((tail.at[k], dst.at[pl.ds(0, TAIL), lanes]))
    return places


def project_kernel(n_proj, n_out, width, *refs):
    pieces = refs[:8]
    tail, *weights, taps = refs[8:-6 - n_out]
    outs = refs[-6 - n_out : -6]
    tok, wts, part, tok_sem, tail_sem, w_sems = refs[-6:]
    rows = pieces[0].shape[0]
    total = wts.shape[3]
    chan = total // n_proj
    n_tiles = chan // width
    copies = piece_copies(pieces, tok, TAIL, tok_sem)
    for ref, to in tail_places(tail, tok):
        copies.append(pltpu.make_async_copy(ref, to, tail_sem))
    for copy in copies:
        copy.start()
    w_copies = []
    for tile in range(n_tiles):
        group = []
        for proj in range(n_proj):
            lanes = pl.ds(proj * chan + tile * width, width)
            for src, to in weight_copies(weights, wts, lanes):
                group.append(pltpu.make_async_copy(src, to, w_sems.at[tile]))
        for copy in group:
            copy.start()
        w_copies.append(group)
    for copy in copies:
        copy.wait()
    for tile in range(n_tiles):
        for copy in w_copies[tile]:
            copy.wait()
        smooth = []
        for proj in range(n_proj):
            lanes = pl.ds(proj * chan + tile * width, width)
            weights = wts[:, :, :, lanes].reshape(-1, width)
            product = jnp.dot(tok[...], weights, preferred_element_type=F32)
            part[proj] = product.astype(BF16).astype(F32)
            cols = pl.ds(tile * width, width)
            value = taps[proj, 0:1, cols] * part[proj, pl.ds(TAIL, rows), :]
            value = value + taps[proj, 1:2, cols] * part[proj, pl.ds(TAIL - 1, rows), :]
            value = value + taps[proj, 2:3, cols] * part[proj, pl.ds(TAIL - 2, rows), :]
            smooth.append(value)
        cols = pl.ds(tile * width, width)
        if n_proj == 1:
            outs[0][:, cols] = smooth[0]
        else:
            mixed = smooth[0] * smooth[1]
            outs[0][:, cols] = mixed.astype(BF16)
            turned = mixed.T.astype(BF16)
            for a in range(2):
                block = turned[:, 256 * a : 256 * a + 256].reshape(width // 16, 16, 256)
                outs[1][pl.ds(tile * (width // 16), width // 16), pl.ds(16 * a, 16), :] = block


def project(pieces, tail, weights, taps, out_shapes):
    n_proj = taps.shape[0]
    total = weights[0].shape[-1]
    width = 256
    n_tiles = total // n_proj // width
    rows = pieces[0].shape[0]
    depth = TP * pieces[0].shape[1]
    return pl.pallas_call(
        functools.partial(project_kernel, n_proj, len(out_shapes), width),
        out_shape=out_shapes,
        in_specs=[HBM] * (9 + len(weights)) + [VMEM],
        out_specs=[VMEM] * len(out_shapes),
        scratch_shapes=[
            pltpu.VMEM((TAIL + rows, depth), BF16),
            pltpu.VMEM((NZ, 4, depth // CTX, total), BF16),
            pltpu.VMEM((n_proj, TAIL + rows, width), F32),
            pltpu.SemaphoreType.DMA,
            pltpu.SemaphoreType.DMA,
            pltpu.SemaphoreType.DMA((n_tiles,)),
        ],
        compiler_params=pltpu.CompilerParams(vmem_limit_bytes=60 * MIB),
        name="project%d" % n_proj,
    )(*pieces, tail, *weights, taps)


def toeplitz_kernel(mine, other, out_hbm, out_ref, rows_ref, seg_ref, row_sem, sem):
    _, y, core = weight_slots()
    group = lax.axis_index("ctx")
    width = rows_ref.shape[3]
    lanes = pl.ds(pl.multiple_of(group // 16 * width, width), width)
    filter_rows = pl.ds(mine.shape[2] - 16, 16)
    copies = []
    for dc, ref in enumerate((mine, other)):
        for dy in (0, 1):
            slot = ((y + dy) % 2) * 2 + (core + dc) % 2
            src = ref.at[:, dy, filter_rows, lanes]
            copies.append(pltpu.make_async_copy(src, rows_ref.at[:, slot], row_sem))
    for copy in copies:
        copy.start()
    for copy in copies:
        copy.wait()
    chosen = lax.broadcasted_iota(jnp.int32, (16, width), 0) == group % 16
    for k in range(CTX):
        block = rows_ref[k // 4, k % 4].astype(F32)
        row = jnp.sum(jnp.where(chosen, block, 0.0), axis=0, keepdims=True)
        for q in range(4):
            seg_ref[4 * k + q : 4 * k + q + 1, :] = row[:, 128 * q : 128 * q + 128]
    low = lax.broadcasted_iota(jnp.int32, (128, 128), 1) >= lax.broadcasted_iota(
        jnp.int32, (128, 128), 0
    )

    def turn(m):
        row = jnp.broadcast_to(seg_ref[pl.ds(m, 1), :], (128, 128))
        return pltpu.roll(row, 0, 1, stride=1, stride_axis=0)

    def body(d, before):
        even = turn(2 * d)
        odd = turn(2 * d + 1)
        same = jnp.where(low, even, before).astype(BF16)
        second = jnp.where(low, odd, even).astype(BF16)
        out_ref[d, 0:128, 0:128] = same
        out_ref[d, 128:256, 128:256] = same
        out_ref[d, 0:128, 128:256] = second
        out_ref[d + 1, 128:256, 0:128] = second
        return odd

    def copy_out(g):
        here = pl.ds(g * 8, 8)
        return pltpu.make_async_copy(out_ref.at[here], out_hbm.at[here], sem.at[g])

    out_ref[0, 128:256, 0:128] = jnp.zeros((128, 128), BF16)
    before = jnp.zeros((128, 128), F32)
    for g in range(8):
        before = lax.fori_loop(g * 8, g * 8 + 8, body, before)
        copy_out(g).start()
    for g in range(8):
        copy_out(g).wait()


def toeplitz(weights):
    return pl.pallas_call(
        toeplitz_kernel,
        out_shape=jax.ShapeDtypeStruct((64, 256, 256), BF16),
        in_specs=[HBM] * 2,
        out_specs=HBM,
        scratch_shapes=[
            pltpu.VMEM((65, 256, 256), BF16),
            pltpu.VMEM((NZ, 4, 16, 512), BF16),
            pltpu.VMEM((128, 128), F32),
            pltpu.SemaphoreType.DMA,
            pltpu.SemaphoreType.DMA((8,)),
        ],
        compiler_params=pltpu.CompilerParams(vmem_limit_bytes=60 * MIB),
        name="toeplitz",
    )(*weights)


TILE = 128
LAGS = TILE // 16
FETCHES = 4


def conv_kernel(x_ref, h_hbm, y_ref, h_ref, sems):
    rows, width = x_ref.shape
    tiles = rows // TILE

    def fetch(g):
        count = h_ref.shape[0] // FETCHES
        here = pl.ds(g * count, count)
        return pltpu.make_async_copy(h_hbm.at[here], h_ref.at[here], sems.at[g])

    for g in range(FETCHES):
        fetch(g).start()
    for tile in range(tiles):
        if tile % (tiles // FETCHES) == 0:
            fetch(tile // (tiles // FETCHES)).wait()
        lags = (tile + 1) * LAGS
        shifted = []
        for lag in range(lags):
            first = tile * TILE - 16 * lag
            if first >= 0:
                shifted.append(x_ref[first : first + TILE, :])
            else:
                empty = jnp.zeros((-first, width), BF16)
                shifted.append(jnp.concatenate([empty, x_ref[0 : TILE + first, :]], axis=0))
        product = jnp.dot(
            jnp.concatenate(shifted, axis=1),
            h_ref[0 : lags * width, :],
            preferred_element_type=F32,
        )
        y_ref[tile * TILE : tile * TILE + TILE, :] = product.astype(BF16)


def conv(x, table):
    rows, width = x.shape
    return pl.pallas_call(
        conv_kernel,
        out_shape=jax.ShapeDtypeStruct((rows, width), BF16),
        in_specs=[VMEM, HBM],
        out_specs=VMEM,
        scratch_shapes=[
            pltpu.VMEM((64 * width, width), BF16),
            pltpu.SemaphoreType.DMA((FETCHES,)),
        ],
        compiler_params=pltpu.CompilerParams(vmem_limit_bytes=60 * MIB),
        name="conv",
    )(x, table.reshape(64 * width, width))


def gate_kernel(back_ref, mixed_ref, query_ref, skip_ref, out_ref):
    chan = mixed_ref.shape[1]
    for a in range(2):
        block = back_ref[:, 16 * a : 16 * a + 16, :].reshape(chan, 256)
        turned = block.astype(F32).T
        here = pl.ds(256 * a, 256)
        mixed = mixed_ref[here, :].astype(F32)
        out_ref[here, :] = (query_ref[here, :] * (turned + skip_ref[...] * mixed)).astype(BF16)


def gate(back, mixed, query, skip):
    return pl.pallas_call(
        gate_kernel,
        out_shape=jax.ShapeDtypeStruct(mixed.shape, BF16),
        in_specs=[VMEM] * 4,
        out_specs=VMEM,
        compiler_params=pltpu.CompilerParams(vmem_limit_bytes=8 * MIB),
        name="gate",
    )(back, mixed, query, skip)


def near_parts(pieces):
    me = lax.axis_index("tp")
    x, y = me // 2, me % 2
    offsets = [(0, 0), (0, 1), (-1, 0), (1, 0), (-1, 1), (1, 1)]
    rows = pieces[0].shape[0]
    parts = []
    for k, (dx, dy) in enumerate(offsets):
        there = ((x + dx + NX) % NX) * 2 + (y + dy) % 2
        parts.append((there, [(pieces[k], 0), (pieces[6 + k], rows)]))
    return parts


def far_parts(pieces):
    me = lax.axis_index("tp")
    x, y = me // 2, me % 2
    count = pieces[0].shape[0] // 2
    parts = []
    for dy in (0, 1):
        rows = pl.ds(dy * count, count)
        there = ((x + 2) % NX) * 2 + (y + dy) % 2
        sources = [(piece.at[rows], k * count) for k, piece in enumerate(pieces)]
        parts.append((there, sources))
    return parts


def output_kernel(parts_of, n_pieces, *refs):
    pieces, (weights, *start) = refs[:n_pieces], refs[n_pieces:-4]
    out_ref, act, wts, sem = refs[-4:]
    _, y, core = weight_slots()
    width = weights.shape[3]
    depth = wts.shape[1]
    copies = []
    for p, (there, sources) in enumerate(parts_of(pieces)):
        for src, first in sources:
            to = act.at[pl.ds(first, src.shape[0]), pl.ds(p * depth, depth)]
            copies.append(pltpu.make_async_copy(src, to, sem))
        for k in range(4):
            slot = ((y + k // 2) % 2) * 2 + (core + k % 2) % 2
            lanes = pl.ds(pl.multiple_of(slot * width, width), width)
            to = wts.at[p, :, lanes]
            copies.append(pltpu.make_async_copy(weights.at[there, k], to, sem))
    for copy in copies:
        copy.start()
    for copy in copies:
        copy.wait()
    matrix = wts[...].reshape(-1, wts.shape[2])
    total = jnp.dot(act[...], matrix, preferred_element_type=F32)
    if start:
        total = total + start[0][...]
    out_ref[...] = total.astype(out_ref.dtype)


def output(pieces, parts_of, parts, weights, start, dtype):
    rows = 2 * pieces[0].shape[0]
    depth, width = weights.shape[2:]
    return pl.pallas_call(
        functools.partial(output_kernel, parts_of, len(pieces)),
        out_shape=jax.ShapeDtypeStruct((rows, 4 * width), dtype),
        in_specs=[HBM] * (len(pieces) + 1) + [VMEM] * len(start),
        out_specs=VMEM,
        scratch_shapes=[
            pltpu.VMEM((rows, parts * depth), BF16),
            pltpu.VMEM((parts, depth, 4 * width), BF16),
            pltpu.SemaphoreType.DMA,
        ],
        compiler_params=pltpu.CompilerParams(vmem_limit_bytes=60 * MIB),
        name="output%d" % parts,
    )(*pieces, weights, *start)


def pair_ylo(own):
    return jnp.stack([own, swap_ylo(own)])


def local(tokens, w_in, short_taps, filters, skip, w_out):
    rows, _ = tokens.shape
    depth, chan = w_in.shape[1:]
    taps = short_taps.transpose(0, 2, 1)

    kv = jnp.concatenate([w_in[1], w_in[2]], axis=1)
    filt = jnp.concatenate([filters[:16], filters[16:]], axis=1)
    kv_mine = gather_z(pair_ylo(jnp.concatenate([kv, filt])))
    route = []
    for z in range(NZ):
        for r in range(4):
            for j in range(TP):
                route.append(((4 * z + r) * TP + j, (4 * j + r) * TP + z))
    w_out = lax.ppermute(w_out, ("ctx", "tp"), route)
    pieces, w_out = gather_tp(tokens, w_out)
    tail = last_rows(pieces)
    tail = lax.ppermute(tail, "ctx", [(i, i + 1) for i in range(CTX - 1)])

    kv_mine, tail, *pieces = barrier(kv_mine, tail, *pieces)
    w_in, kv_mine = barrier(w_in, kv_mine)
    kv_other = swap_core(kv_mine)
    q_mine = gather_z(pair_ylo(w_in[0]))
    mixed, blocks = project(
        pieces,
        tail,
        (kv_mine, kv_other),
        taps[1:],
        [
            jax.ShapeDtypeStruct((rows, chan), BF16),
            jax.ShapeDtypeStruct((CTX, 32, 256), BF16),
        ],
    )

    w_out, blocks = barrier(w_out, blocks)
    o_pair = jnp.stack([w_out, swap_core(w_out)])
    o_pair = jnp.concatenate([o_pair, swap_ylo(o_pair)])
    sent = lax.all_to_all(blocks, "ctx", 0, 0, tiled=True)
    table = toeplitz((kv_mine, kv_other))
    o_pair, sent, table = barrier(o_pair, sent, table)
    result = conv(sent.reshape(CTX * 32, 256), table)
    q_mine, o_pair, result = barrier(q_mine, o_pair, result)
    back = lax.all_to_all(result.reshape(CTX, 32, 256), "ctx", 0, 0, tiled=True)
    o_mine = gather_z(o_pair)
    (query,) = project(
        pieces,
        tail,
        (q_mine, swap_core(q_mine)),
        taps[:1],
        [jax.ShapeDtypeStruct((rows, chan), F32)],
    )
    gated = gate(back, mixed, query, skip[None, :])

    half = rows // 2
    first, second = gather_tp(gated[:half])[0], gather_tp(gated[half:])[0]
    total = output(first[:6] + second[:6], near_parts, 6, o_mine, [], F32)
    return output(first[6:] + second[6:], far_parts, 2, o_mine, [total], BF16)


def solution(mesh):
    return jax.shard_map(
        local,
        mesh=mesh,
        in_specs=(
            P("ctx", "tp"),
            P(None, "ctx", "tp"),
            P(None, "tp", None),
            P("tp", "ctx"),
            P("tp"),
            P("tp", "ctx"),
        ),
        out_specs=P("ctx", "tp"),
        check_vma=False,
    )
```

```python
import functools

import jax
import jax.numpy as jnp
from jax import lax
from jax.experimental import pallas as pl
from jax.experimental.pallas import tpu as pltpu
from jax.sharding import PartitionSpec as P

F32 = jnp.float32
BF16 = jnp.bfloat16
HBM = pl.BlockSpec(memory_space=pltpu.HBM)
VMEM = pl.BlockSpec(memory_space=pltpu.VMEM)
MIB = 1024 * 1024

NZ, NX = 8, 4
CTX = NZ * 4
TP = NX * 2
TAIL = 16


def barrier(*arrays):
    return lax.optimization_barrier(arrays)


def shift_z(block, step):
    route = [(i, (i + 4 * step) % CTX) for i in range(CTX)]
    return lax.ppermute(block, "ctx", route)


def swap_ctx(block, mask):
    return lax.ppermute(block, "ctx", [(i, i ^ mask) for i in range(CTX)])


def swap_core(block):
    return swap_ctx(block, 1)


def swap_ylo(block):
    return swap_ctx(block, 2)


def shift_x(block, step):
    route = [(j, (j + 2 * step) % TP) for j in range(TP)]
    return lax.ppermute(block, "tp", route)


def swap_yhi(block):
    return lax.ppermute(block, "tp", [(j, j ^ 1) for j in range(TP)])


def gather_z(block):
    groups = [[4 * z + rest for z in range(NZ)] for rest in range(4)]
    return lax.all_gather(block, "ctx", axis=0, tiled=False, axis_index_groups=groups)


def gather_tp(own, first=None):
    half = own.shape[0] // 2
    near = swap_yhi(own)
    if first is not None:
        near, first = barrier(near, first)
    own_right, own_left = shift_x(own, 1), shift_x(own, -1)
    near_right, near_left = shift_x(near, 1), shift_x(near, -1)
    far_right = shift_x(jnp.concatenate([own_right[:half], near_right[:half]]), 1)
    far_left = shift_x(jnp.concatenate([own_left[half:], near_left[half:]]), -1)
    pieces = [own, near, own_right, own_left, near_right, near_left, far_right, far_left]
    return pieces, first


def piece_copies(pieces, dst, first_row, sem):
    me = lax.axis_index("tp")
    x, y = me // 2, me % 2
    width = pieces[0].shape[1]
    rows = pieces[0].shape[0]
    half = rows // 2

    def place(dx, dy, begin, count):
        there = ((x + dx + NX) % NX) * 2 + (y + dy) % 2
        lanes = pl.ds(pl.multiple_of(there * width, width), width)
        return dst.at[pl.ds(first_row + begin, count), lanes]

    whole = [(0, 0), (0, 1), (-1, 0), (1, 0), (-1, 1), (1, 1)]
    copies = []
    for ref, (dx, dy) in zip(pieces[:6], whole):
        copies.append((ref, place(dx, dy, 0, rows)))
    for ref, begin in ((pieces[6], 0), (pieces[7], half)):
        for dy in (0, 1):
            copies.append((ref.at[pl.ds(dy * half, half)], place(2, dy, begin, half)))
    return [pltpu.make_async_copy(src, to, sem) for src, to in copies]


def weight_slots():
    me = lax.axis_index("ctx")
    return me // 4, (me // 2) % 2, me % 2


def weight_copies(weights, proj, cols, dst):
    _, y, core = weight_slots()
    copies = []
    for dc, ref in enumerate(weights):
        for dy in (0, 1):
            slot = ((y + dy) % 2) * 2 + (core + dc) % 2
            src = ref.at[:, dy, proj, pl.ds(0, dst.shape[2]), cols]
            copies.append((src, dst.at[:, slot]))
    return copies


def pack_kernel(moves, *refs):
    *sources, out, sem = refs
    copies = [
        pltpu.make_async_copy(sources[k].at[src], out.at[dst], sem) for k, src, dst in moves
    ]
    for copy in copies:
        copy.start()
    for copy in copies:
        copy.wait()


def pack(sources, shape, moves, name):
    return pl.pallas_call(
        functools.partial(pack_kernel, moves),
        out_shape=jax.ShapeDtypeStruct(shape, sources[0].dtype),
        in_specs=[HBM] * len(sources),
        out_specs=VMEM,
        scratch_shapes=[pltpu.SemaphoreType.DMA],
        compiler_params=pltpu.CompilerParams(vmem_limit_bytes=8 * MIB),
        name=name,
    )(*sources)


def last_rows(pieces):
    rows, width = pieces[0].shape
    half = rows // 2
    moves = [(k, (pl.ds(rows - TAIL, TAIL),), (k,)) for k in range(6)]
    moves.append((6, (pl.ds(half - TAIL, TAIL),), (6,)))
    moves.append((6, (pl.ds(rows - TAIL, TAIL),), (7,)))
    return pack([*pieces[:6], pieces[7]], (TP, TAIL, width), moves, "tail")


def tail_places(tail, dst):
    me = lax.axis_index("tp")
    x, y = me // 2, me % 2
    width = tail.shape[2]
    offsets = [(0, 0), (0, 1), (-1, 0), (1, 0), (-1, 1), (1, 1), (2, 0), (2, 1)]
    places = []
    for k, (dx, dy) in enumerate(offsets):
        there = ((x + dx + NX) % NX) * 2 + (y + dy) % 2
        lanes = pl.ds(pl.multiple_of(there * width, width), width)
        places.append((tail.at[k], dst.at[pl.ds(0, TAIL), lanes]))
    return places


def project_kernel(n_proj, n_out, width, *refs):
    pieces = refs[:8]
    tail, *weights, taps = refs[8:-6 - n_out]
    outs = refs[-6 - n_out : -6]
    tok, wts, part, tok_sem, tail_sem, w_sems = refs[-6:]
    rows = pieces[0].shape[0]
    total = wts.shape[3]
    chan = total // n_proj
    n_tiles = chan // width
    copies = piece_copies(pieces, tok, TAIL, tok_sem)
    for ref, to in tail_places(tail, tok):
        copies.append(pltpu.make_async_copy(ref, to, tail_sem))
    for copy in copies:
        copy.start()
    w_copies = []
    for tile in range(n_tiles):
        group = []
        for proj in range(n_proj):
            lanes = pl.ds(proj * chan + tile * width, width)
            cols = pl.ds(tile * width, width)
            for src, to in weight_copies(weights, proj, cols, wts.at[:, :, :, lanes]):
                group.append(pltpu.make_async_copy(src, to, w_sems.at[tile]))
        for copy in group:
            copy.start()
        w_copies.append(group)
    for copy in copies:
        copy.wait()
    for tile in range(n_tiles):
        for copy in w_copies[tile]:
            copy.wait()
        smooth = []
        for proj in range(n_proj):
            lanes = pl.ds(proj * chan + tile * width, width)
            weights = wts[:, :, :, lanes].reshape(-1, width)
            product = jnp.dot(tok[...], weights, preferred_element_type=F32)
            part[proj] = product.astype(BF16).astype(F32)
            cols = pl.ds(tile * width, width)
            value = taps[proj, 0:1, cols] * part[proj, pl.ds(TAIL, rows), :]
            value = value + taps[proj, 1:2, cols] * part[proj, pl.ds(TAIL - 1, rows), :]
            value = value + taps[proj, 2:3, cols] * part[proj, pl.ds(TAIL - 2, rows), :]
            smooth.append(value)
        cols = pl.ds(tile * width, width)
        if n_proj == 1:
            outs[0][:, cols] = smooth[0]
        else:
            mixed = smooth[0] * smooth[1]
            outs[0][:, cols] = mixed.astype(BF16)
            turned = mixed.T.astype(BF16)
            for a in range(2):
                block = turned[:, 256 * a : 256 * a + 256].reshape(width // 16, 16, 256)
                outs[1][pl.ds(tile * (width // 16), width // 16), pl.ds(16 * a, 16), :] = block


def project(pieces, tail, weights, taps, out_shapes):
    n_proj = taps.shape[0]
    total = weights[0].shape[-1] * n_proj
    width = 256
    n_tiles = total // n_proj // width
    rows = pieces[0].shape[0]
    depth = TP * pieces[0].shape[1]
    return pl.pallas_call(
        functools.partial(project_kernel, n_proj, len(out_shapes), width),
        out_shape=out_shapes,
        in_specs=[HBM] * (9 + len(weights)) + [VMEM],
        out_specs=[VMEM] * len(out_shapes),
        scratch_shapes=[
            pltpu.VMEM((TAIL + rows, depth), BF16),
            pltpu.VMEM((NZ, 4, depth // CTX, total), BF16),
            pltpu.VMEM((n_proj, TAIL + rows, width), F32),
            pltpu.SemaphoreType.DMA,
            pltpu.SemaphoreType.DMA,
            pltpu.SemaphoreType.DMA((n_tiles,)),
        ],
        compiler_params=pltpu.CompilerParams(vmem_limit_bytes=60 * MIB),
        name="project%d" % n_proj,
    )(*pieces, tail, *weights, taps)


def toeplitz_kernel(mine, other, out_hbm, out_ref, rows_ref, seg_ref, row_sem, sem):
    _, y, core = weight_slots()
    group = lax.axis_index("ctx")
    width = rows_ref.shape[3]
    filter_rows = pl.ds(mine.shape[3] - 16, 16)
    copies = []
    for dc, ref in enumerate((mine, other)):
        for dy in (0, 1):
            slot = ((y + dy) % 2) * 2 + (core + dc) % 2
            src = ref.at[:, dy, group // 16, filter_rows]
            copies.append(pltpu.make_async_copy(src, rows_ref.at[:, slot], row_sem))
    for copy in copies:
        copy.start()
    for copy in copies:
        copy.wait()
    chosen = lax.broadcasted_iota(jnp.int32, (16, width), 0) == group % 16
    for k in range(CTX):
        block = rows_ref[k // 4, k % 4].astype(F32)
        row = jnp.sum(jnp.where(chosen, block, 0.0), axis=0, keepdims=True)
        for q in range(4):
            seg_ref[4 * k + q : 4 * k + q + 1, :] = row[:, 128 * q : 128 * q + 128]
    low = lax.broadcasted_iota(jnp.int32, (128, 128), 1) >= lax.broadcasted_iota(
        jnp.int32, (128, 128), 0
    )

    def turn(m):
        row = jnp.broadcast_to(seg_ref[pl.ds(m, 1), :], (128, 128))
        return pltpu.roll(row, 0, 1, stride=1, stride_axis=0)

    def body(d, before):
        even = turn(2 * d)
        odd = turn(2 * d + 1)
        same = jnp.where(low, even, before).astype(BF16)
        second = jnp.where(low, odd, even).astype(BF16)
        out_ref[d, 0:128, 0:128] = same
        out_ref[d, 128:256, 128:256] = same
        out_ref[d, 0:128, 128:256] = second
        out_ref[d + 1, 128:256, 0:128] = second
        return odd

    def copy_out(g):
        here = pl.ds(g * 8, 8)
        return pltpu.make_async_copy(out_ref.at[here], out_hbm.at[here], sem.at[g])

    out_ref[0, 128:256, 0:128] = jnp.zeros((128, 128), BF16)
    before = jnp.zeros((128, 128), F32)
    for g in range(8):
        before = lax.fori_loop(g * 8, g * 8 + 8, body, before)
        copy_out(g).start()
    for g in range(8):
        copy_out(g).wait()


def toeplitz(weights):
    return pl.pallas_call(
        toeplitz_kernel,
        out_shape=jax.ShapeDtypeStruct((64, 256, 256), BF16),
        in_specs=[HBM] * 2,
        out_specs=HBM,
        scratch_shapes=[
            pltpu.VMEM((65, 256, 256), BF16),
            pltpu.VMEM((NZ, 4, 16, 512), BF16),
            pltpu.VMEM((128, 128), F32),
            pltpu.SemaphoreType.DMA,
            pltpu.SemaphoreType.DMA((8,)),
        ],
        compiler_params=pltpu.CompilerParams(vmem_limit_bytes=60 * MIB),
        name="toeplitz",
    )(*weights)


TILE = 128
LAGS = TILE // 16
FETCHES = 4


def conv_kernel(x_hbm, h_hbm, y_ref, x_ref, h_ref, acc, x_sem, sems):
    rows, width = x_ref.shape
    tiles = rows // TILE
    count = h_ref.shape[0] // FETCHES
    lags = count // width

    def fetch(g):
        here = pl.ds(g * count, count)
        return pltpu.make_async_copy(h_hbm.at[here], h_ref.at[here], sems.at[g])

    x_copy = pltpu.make_async_copy(x_hbm, x_ref, x_sem)
    x_copy.start()
    for g in range(FETCHES):
        fetch(g).start()
    x_copy.wait()
    for g in range(FETCHES):
        fetch(g).wait()
        for tile in range(tiles):
            last = (tile + 1) * LAGS
            shifted = []
            for lag in range(g * lags, min(g * lags + lags, last)):
                first = tile * TILE - 16 * lag
                if first >= 0:
                    shifted.append(x_ref[first : first + TILE, :])
                else:
                    empty = jnp.zeros((-first, width), BF16)
                    shifted.append(jnp.concatenate([empty, x_ref[0 : TILE + first, :]], axis=0))
            if not shifted:
                continue
            begin = g * count
            product = jnp.dot(
                jnp.concatenate(shifted, axis=1),
                h_ref[begin : begin + len(shifted) * width, :],
                preferred_element_type=F32,
            )
            here = slice(tile * TILE, tile * TILE + TILE)
            if g:
                product = product + acc[here, :]
            if g * lags + lags >= last:
                y_ref[here, :] = product.astype(BF16)
            else:
                acc[here, :] = product


def conv(x, table):
    rows, width = x.shape
    return pl.pallas_call(
        conv_kernel,
        out_shape=jax.ShapeDtypeStruct((rows, width), BF16),
        in_specs=[HBM, HBM],
        out_specs=VMEM,
        scratch_shapes=[
            pltpu.VMEM((rows, width), BF16),
            pltpu.VMEM((64 * width, width), BF16),
            pltpu.VMEM((rows, width), F32),
            pltpu.SemaphoreType.DMA,
            pltpu.SemaphoreType.DMA((FETCHES,)),
        ],
        compiler_params=pltpu.CompilerParams(vmem_limit_bytes=60 * MIB),
        name="conv",
    )(x, table.reshape(64 * width, width))


def gate_kernel(half, back_ref, mixed_ref, query_ref, skip_ref, out_ref):
    rows, chan = out_ref.shape
    here = pl.ds(half * rows, rows)
    block = back_ref[:, 16 * half : 16 * half + 16, :].reshape(chan, rows)
    turned = block.astype(F32).T
    mixed = mixed_ref[here, :].astype(F32)
    out_ref[...] = (query_ref[here, :] * (turned + skip_ref[...] * mixed)).astype(BF16)


def gate(back, mixed, query, skip, half):
    return pl.pallas_call(
        functools.partial(gate_kernel, half),
        out_shape=jax.ShapeDtypeStruct((back.shape[2], mixed.shape[1]), BF16),
        in_specs=[VMEM] * 4,
        out_specs=VMEM,
        compiler_params=pltpu.CompilerParams(vmem_limit_bytes=8 * MIB),
        name="gate%d" % half,
    )(back, mixed, query, skip)


def near_parts(pieces):
    me = lax.axis_index("tp")
    x, y = me // 2, me % 2
    offsets = [(0, 0), (0, 1), (-1, 0), (1, 0), (-1, 1), (1, 1)]
    rows = pieces[0].shape[0]
    parts = []
    for k, (dx, dy) in enumerate(offsets):
        there = ((x + dx + NX) % NX) * 2 + (y + dy) % 2
        parts.append((there, [(pieces[k], 0), (pieces[6 + k], rows)]))
    return parts


def far_parts(pieces):
    me = lax.axis_index("tp")
    x, y = me // 2, me % 2
    count = pieces[0].shape[0] // 2
    parts = []
    for dy in (0, 1):
        rows = pl.ds(dy * count, count)
        there = ((x + 2) % NX) * 2 + (y + dy) % 2
        sources = [(piece.at[rows], k * count) for k, piece in enumerate(pieces)]
        parts.append((there, sources))
    return parts


def output_kernel(parts_of, n_pieces, *refs):
    pieces, (weights, *start) = refs[:n_pieces], refs[n_pieces:-5]
    out_ref, act, wts, before, sem = refs[-5:]
    _, y, core = weight_slots()
    width = weights.shape[3]
    depth = wts.shape[1]
    copies = []
    for p, (there, sources) in enumerate(parts_of(pieces)):
        for src, first in sources:
            to = act.at[pl.ds(first, src.shape[0]), pl.ds(p * depth, depth)]
            copies.append(pltpu.make_async_copy(src, to, sem))
        for k in range(4):
            slot = ((y + k // 2) % 2) * 2 + (core + k % 2) % 2
            lanes = pl.ds(pl.multiple_of(slot * width, width), width)
            to = wts.at[p, :, lanes]
            copies.append(pltpu.make_async_copy(weights.at[there, k], to, sem))
    if start:
        copies.append(pltpu.make_async_copy(start[0], before, sem))
    for copy in copies:
        copy.start()
    for copy in copies:
        copy.wait()
    matrix = wts[...].reshape(-1, wts.shape[2])
    total = jnp.dot(act[...], matrix, preferred_element_type=F32)
    if start:
        total = total + before[...]
    out_ref[...] = total.astype(out_ref.dtype)


def output(pieces, parts_of, parts, weights, start, dtype):
    rows = 2 * pieces[0].shape[0]
    depth, width = weights.shape[2:]
    return pl.pallas_call(
        functools.partial(output_kernel, parts_of, len(pieces)),
        out_shape=jax.ShapeDtypeStruct((rows, 4 * width), dtype),
        in_specs=[HBM] * (len(pieces) + 1 + len(start)),
        out_specs=VMEM,
        scratch_shapes=[
            pltpu.VMEM((rows, parts * depth), BF16),
            pltpu.VMEM((parts, depth, 4 * width), BF16),
            pltpu.VMEM((rows, 4 * width) if start else (8, 128), F32),
            pltpu.SemaphoreType.DMA,
        ],
        compiler_params=pltpu.CompilerParams(vmem_limit_bytes=60 * MIB),
        name="output%d" % parts,
    )(*pieces, weights, *start)


def pair_ylo(own):
    return jnp.stack([own, swap_ylo(own)])


def local(tokens, w_in, short_taps, filters, skip, w_out):
    rows, _ = tokens.shape
    depth, chan = w_in.shape[1:]
    taps = short_taps.transpose(0, 2, 1)

    kv = jnp.concatenate([w_in[1:], filters.reshape(2, 16, -1)], axis=1)
    kv_mine = gather_z(pair_ylo(kv))
    route = []
    for z in range(NZ):
        for r in range(4):
            for j in range(TP):
                route.append(((4 * z + r) * TP + j, (4 * j + r) * TP + z))
    w_out = lax.ppermute(w_out, ("ctx", "tp"), route)
    pieces, w_out = gather_tp(tokens, w_out)
    tail = last_rows(pieces)
    tail = lax.ppermute(tail, "ctx", [(i, i + 1) for i in range(CTX - 1)])

    kv_mine, tail, *pieces = barrier(kv_mine, tail, *pieces)
    w_in, kv_mine = barrier(w_in, kv_mine)
    kv_other = swap_core(kv_mine)
    q_mine = gather_z(pair_ylo(w_in[:1]))
    mixed, blocks = project(
        pieces,
        tail,
        (kv_mine, kv_other),
        taps[1:],
        [
            jax.ShapeDtypeStruct((rows, chan), BF16),
            jax.ShapeDtypeStruct((CTX, 32, 256), BF16),
        ],
    )

    w_out, blocks = barrier(w_out, blocks)
    o_pair = jnp.stack([w_out, swap_core(w_out)])
    o_pair = jnp.concatenate([o_pair, swap_ylo(o_pair)])
    sent = lax.all_to_all(blocks, "ctx", 0, 0, tiled=True)
    table = toeplitz((kv_mine, kv_other))
    o_pair, sent, table = barrier(o_pair, sent, table)
    result = conv(sent.reshape(CTX * 32, 256), table)
    q_mine, o_pair, result = barrier(q_mine, o_pair, result)
    back = lax.all_to_all(result.reshape(CTX, 32, 256), "ctx", 0, 0, tiled=True)
    o_mine = gather_z(o_pair)
    (query,) = project(
        pieces,
        tail,
        (q_mine, swap_core(q_mine)),
        taps[:1],
        [jax.ShapeDtypeStruct((rows, chan), F32)],
    )
    gated = [gate(back, mixed, query, skip[None, :], half) for half in range(2)]

    first, second = gather_tp(gated[0])[0], gather_tp(gated[1])[0]
    total = output(first[:6] + second[:6], near_parts, 6, o_mine, [], F32)
    return output(first[6:] + second[6:], far_parts, 2, o_mine, [total], BF16)


def solution(mesh):
    return jax.shard_map(
        local,
        mesh=mesh,
        in_specs=(
            P("ctx", "tp"),
            P(None, "ctx", "tp"),
            P(None, "tp", None),
            P("tp", "ctx"),
            P("tp"),
            P("tp", "ctx"),
        ),
        out_specs=P("ctx", "tp"),
        check_vma=False,
    )
```

```python
import functools

import jax
import jax.numpy as jnp
from jax import lax
from jax.experimental import pallas as pl
from jax.experimental.pallas import tpu as pltpu
from jax.sharding import PartitionSpec as P

F32 = jnp.float32
BF16 = jnp.bfloat16
HBM = pl.BlockSpec(memory_space=pltpu.HBM)
VMEM = pl.BlockSpec(memory_space=pltpu.VMEM)
MIB = 1024 * 1024

NZ, NX = 8, 4
CTX = NZ * 4
TP = NX * 2
TAIL = 16


def barrier(*arrays):
    return lax.optimization_barrier(arrays)


def shift_z(block, step):
    route = [(i, (i + 4 * step) % CTX) for i in range(CTX)]
    return lax.ppermute(block, "ctx", route)


def swap_ctx(block, mask):
    return lax.ppermute(block, "ctx", [(i, i ^ mask) for i in range(CTX)])


def swap_core(block):
    return swap_ctx(block, 1)


def swap_ylo(block):
    return swap_ctx(block, 2)


def shift_x(block, step):
    route = [(j, (j + 2 * step) % TP) for j in range(TP)]
    return lax.ppermute(block, "tp", route)


def swap_yhi(block):
    return lax.ppermute(block, "tp", [(j, j ^ 1) for j in range(TP)])


def gather_z(block):
    groups = [[4 * z + rest for z in range(NZ)] for rest in range(4)]
    return lax.all_gather(block, "ctx", axis=0, tiled=False, axis_index_groups=groups)


def gather_tp(own, first=None):
    half = own.shape[0] // 2
    near = swap_yhi(own)
    if first is not None:
        near, first = barrier(near, first)
    own_right, own_left = shift_x(own, 1), shift_x(own, -1)
    near_right, near_left = shift_x(near, 1), shift_x(near, -1)
    far_right = shift_x(jnp.concatenate([own_right[:half], near_right[:half]]), 1)
    far_left = shift_x(jnp.concatenate([own_left[half:], near_left[half:]]), -1)
    pieces = [own, near, own_right, own_left, near_right, near_left, far_right, far_left]
    return pieces, first


def piece_copies(pieces, dst, first_row, sem):
    me = lax.axis_index("tp")
    x, y = me // 2, me % 2
    width = pieces[0].shape[1]
    rows = pieces[0].shape[0]
    half = rows // 2

    def place(dx, dy, begin, count):
        there = ((x + dx + NX) % NX) * 2 + (y + dy) % 2
        lanes = pl.ds(pl.multiple_of(there * width, width), width)
        return dst.at[pl.ds(first_row + begin, count), lanes]

    whole = [(0, 0), (0, 1), (-1, 0), (1, 0), (-1, 1), (1, 1)]
    copies = []
    for ref, (dx, dy) in zip(pieces[:6], whole):
        copies.append((ref, place(dx, dy, 0, rows)))
    for ref, begin in ((pieces[6], 0), (pieces[7], half)):
        for dy in (0, 1):
            copies.append((ref.at[pl.ds(dy * half, half)], place(2, dy, begin, half)))
    return [pltpu.make_async_copy(src, to, sem) for src, to in copies]


def weight_slots():
    me = lax.axis_index("ctx")
    return me // 4, (me // 2) % 2, me % 2


def weight_copies(weights, proj, cols, dst):
    _, y, core = weight_slots()
    copies = []
    for dc, ref in enumerate(weights):
        for dy in (0, 1):
            slot = ((y + dy) % 2) * 2 + (core + dc) % 2
            src = ref.at[:, dy, proj, pl.ds(0, dst.shape[2]), cols]
            copies.append((src, dst.at[:, slot]))
    return copies


def pack_kernel(moves, *refs):
    *sources, out, sem = refs
    copies = [
        pltpu.make_async_copy(sources[k].at[src], out.at[dst], sem) for k, src, dst in moves
    ]
    for copy in copies:
        copy.start()
    for copy in copies:
        copy.wait()


def pack(sources, shape, moves, name):
    return pl.pallas_call(
        functools.partial(pack_kernel, moves),
        out_shape=jax.ShapeDtypeStruct(shape, sources[0].dtype),
        in_specs=[HBM] * len(sources),
        out_specs=VMEM,
        scratch_shapes=[pltpu.SemaphoreType.DMA],
        compiler_params=pltpu.CompilerParams(vmem_limit_bytes=8 * MIB),
        name=name,
    )(*sources)


def last_rows(pieces):
    rows, width = pieces[0].shape
    half = rows // 2
    moves = [(k, (pl.ds(rows - TAIL, TAIL),), (k,)) for k in range(6)]
    moves.append((6, (pl.ds(half - TAIL, TAIL),), (6,)))
    moves.append((6, (pl.ds(rows - TAIL, TAIL),), (7,)))
    return pack([*pieces[:6], pieces[7]], (TP, TAIL, width), moves, "tail")


def tail_places(tail, dst):
    me = lax.axis_index("tp")
    x, y = me // 2, me % 2
    width = tail.shape[2]
    offsets = [(0, 0), (0, 1), (-1, 0), (1, 0), (-1, 1), (1, 1), (2, 0), (2, 1)]
    places = []
    for k, (dx, dy) in enumerate(offsets):
        there = ((x + dx + NX) % NX) * 2 + (y + dy) % 2
        lanes = pl.ds(pl.multiple_of(there * width, width), width)
        places.append((tail.at[k], dst.at[pl.ds(0, TAIL), lanes]))
    return places


def project_kernel(n_proj, n_out, width, *refs):
    pieces = refs[:8]
    tail, *weights, taps = refs[8:-6 - n_out]
    outs = refs[-6 - n_out : -6]
    tok, wts, part, tok_sem, tail_sem, w_sems = refs[-6:]
    rows = pieces[0].shape[0]
    total = wts.shape[3]
    chan = total // n_proj
    n_tiles = chan // width
    copies = piece_copies(pieces, tok, TAIL, tok_sem)
    for ref, to in tail_places(tail, tok):
        copies.append(pltpu.make_async_copy(ref, to, tail_sem))
    for copy in copies:
        copy.start()
    w_copies = []
    for tile in range(n_tiles):
        group = []
        for proj in range(n_proj):
            lanes = pl.ds(proj * chan + tile * width, width)
            cols = pl.ds(tile * width, width)
            for src, to in weight_copies(weights, proj, cols, wts.at[:, :, :, lanes]):
                group.append(pltpu.make_async_copy(src, to, w_sems.at[tile]))
        for copy in group:
            copy.start()
        w_copies.append(group)
    for copy in copies:
        copy.wait()
    for tile in range(n_tiles):
        for copy in w_copies[tile]:
            copy.wait()
        smooth = []
        for proj in range(n_proj):
            lanes = pl.ds(proj * chan + tile * width, width)
            weights = wts[:, :, :, lanes].reshape(-1, width)
            product = jnp.dot(tok[...], weights, preferred_element_type=F32)
            part[proj] = product.astype(BF16).astype(F32)
            cols = pl.ds(tile * width, width)
            value = taps[proj, 0:1, cols] * part[proj, pl.ds(TAIL, rows), :]
            value = value + taps[proj, 1:2, cols] * part[proj, pl.ds(TAIL - 1, rows), :]
            value = value + taps[proj, 2:3, cols] * part[proj, pl.ds(TAIL - 2, rows), :]
            smooth.append(value)
        cols = pl.ds(tile * width, width)
        if n_proj == 1:
            outs[0][:, cols] = smooth[0]
        else:
            mixed = smooth[0] * smooth[1]
            outs[0][:, cols] = mixed.astype(BF16)
            turned = mixed.T.astype(BF16)
            for a in range(2):
                block = turned[:, 256 * a : 256 * a + 256].reshape(width // 16, 16, 256)
                outs[1][pl.ds(tile * (width // 16), width // 16), pl.ds(16 * a, 16), :] = block


def project(pieces, tail, weights, taps, out_shapes):
    n_proj = taps.shape[0]
    total = weights[0].shape[-1] * n_proj
    width = 256
    n_tiles = total // n_proj // width
    rows = pieces[0].shape[0]
    depth = TP * pieces[0].shape[1]
    return pl.pallas_call(
        functools.partial(project_kernel, n_proj, len(out_shapes), width),
        out_shape=out_shapes,
        in_specs=[HBM] * (9 + len(weights)) + [VMEM],
        out_specs=[VMEM] * len(out_shapes),
        scratch_shapes=[
            pltpu.VMEM((TAIL + rows, depth), BF16),
            pltpu.VMEM((NZ, 4, depth // CTX, total), BF16),
            pltpu.VMEM((n_proj, TAIL + rows, width), F32),
            pltpu.SemaphoreType.DMA,
            pltpu.SemaphoreType.DMA,
            pltpu.SemaphoreType.DMA((n_tiles,)),
        ],
        compiler_params=pltpu.CompilerParams(vmem_limit_bytes=60 * MIB),
        name="project%d" % n_proj,
    )(*pieces, tail, *weights, taps)


def toeplitz_kernel(mine, other, out_hbm, out_ref, rows_ref, seg_ref, row_sem, sem):
    _, y, core = weight_slots()
    group = lax.axis_index("ctx")
    width = rows_ref.shape[3]
    filter_rows = pl.ds(mine.shape[3] - 16, 16)
    copies = []
    for dc, ref in enumerate((mine, other)):
        for dy in (0, 1):
            slot = ((y + dy) % 2) * 2 + (core + dc) % 2
            src = ref.at[:, dy, group // 16, filter_rows]
            copies.append(pltpu.make_async_copy(src, rows_ref.at[:, slot], row_sem))
    for copy in copies:
        copy.start()
    for copy in copies:
        copy.wait()
    chosen = lax.broadcasted_iota(jnp.int32, (16, width), 0) == group % 16
    for k in range(CTX):
        block = rows_ref[k // 4, k % 4].astype(F32)
        row = jnp.sum(jnp.where(chosen, block, 0.0), axis=0, keepdims=True)
        for q in range(4):
            seg_ref[4 * k + q : 4 * k + q + 1, :] = row[:, 128 * q : 128 * q + 128]
    low = lax.broadcasted_iota(jnp.int32, (128, 128), 1) >= lax.broadcasted_iota(
        jnp.int32, (128, 128), 0
    )

    def turn(m):
        row = jnp.broadcast_to(seg_ref[pl.ds(m, 1), :], (128, 128))
        return pltpu.roll(row, 0, 1, stride=1, stride_axis=0)

    def body(d, before):
        even = turn(2 * d)
        odd = turn(2 * d + 1)
        same = jnp.where(low, even, before).astype(BF16)
        second = jnp.where(low, odd, even).astype(BF16)
        out_ref[d, 0:128, 0:128] = same
        out_ref[d, 128:256, 128:256] = same
        out_ref[d, 0:128, 128:256] = second
        out_ref[d + 1, 128:256, 0:128] = second
        return odd

    def copy_out(g):
        here = pl.ds(g * 8, 8)
        return pltpu.make_async_copy(out_ref.at[here], out_hbm.at[here], sem.at[g])

    out_ref[0, 128:256, 0:128] = jnp.zeros((128, 128), BF16)
    before = jnp.zeros((128, 128), F32)
    for g in range(8):
        before = lax.fori_loop(g * 8, g * 8 + 8, body, before)
        copy_out(g).start()
    for g in range(8):
        copy_out(g).wait()


def toeplitz(weights):
    return pl.pallas_call(
        toeplitz_kernel,
        out_shape=jax.ShapeDtypeStruct((64, 256, 256), BF16),
        in_specs=[HBM] * 2,
        out_specs=HBM,
        scratch_shapes=[
            pltpu.VMEM((65, 256, 256), BF16),
            pltpu.VMEM((NZ, 4, 16, 512), BF16),
            pltpu.VMEM((128, 128), F32),
            pltpu.SemaphoreType.DMA,
            pltpu.SemaphoreType.DMA((8,)),
        ],
        compiler_params=pltpu.CompilerParams(vmem_limit_bytes=60 * MIB),
        name="toeplitz",
    )(*weights)


TILE = 128
LAGS = TILE // 16
FETCHES = 4


def conv_kernel(x_hbm, h_hbm, y_ref, x_ref, h_ref, acc, x_sem, sems):
    rows, width = x_ref.shape
    tiles = rows // TILE
    count = h_ref.shape[0] // FETCHES
    lags = count // width

    def fetch(g):
        here = pl.ds(g * count, count)
        return pltpu.make_async_copy(h_hbm.at[here], h_ref.at[here], sems.at[g])

    x_copy = pltpu.make_async_copy(x_hbm, x_ref, x_sem)
    x_copy.start()
    for g in range(FETCHES):
        fetch(g).start()
    x_copy.wait()
    for g in range(FETCHES):
        fetch(g).wait()
        for tile in range(tiles):
            last = (tile + 1) * LAGS
            shifted = []
            for lag in range(g * lags, min(g * lags + lags, last)):
                first = tile * TILE - 16 * lag
                if first >= 0:
                    shifted.append(x_ref[first : first + TILE, :])
                else:
                    empty = jnp.zeros((-first, width), BF16)
                    shifted.append(jnp.concatenate([empty, x_ref[0 : TILE + first, :]], axis=0))
            if not shifted:
                continue
            begin = g * count
            product = jnp.dot(
                jnp.concatenate(shifted, axis=1),
                h_ref[begin : begin + len(shifted) * width, :],
                preferred_element_type=F32,
            )
            here = slice(tile * TILE, tile * TILE + TILE)
            if g:
                product = product + acc[here, :]
            if g * lags + lags >= last:
                y_ref[here, :] = product.astype(BF16)
            else:
                acc[here, :] = product


def conv(x, table):
    rows, width = x.shape
    return pl.pallas_call(
        conv_kernel,
        out_shape=jax.ShapeDtypeStruct((rows, width), BF16),
        in_specs=[HBM, HBM],
        out_specs=VMEM,
        scratch_shapes=[
            pltpu.VMEM((rows, width), BF16),
            pltpu.VMEM((64 * width, width), BF16),
            pltpu.VMEM((rows, width), F32),
            pltpu.SemaphoreType.DMA,
            pltpu.SemaphoreType.DMA((FETCHES,)),
        ],
        compiler_params=pltpu.CompilerParams(vmem_limit_bytes=60 * MIB),
        name="conv",
    )(x, table.reshape(64 * width, width))


def gate_kernel(half, back_ref, mixed_ref, query_ref, skip_ref, out_ref):
    rows, chan = out_ref.shape
    here = pl.ds(half * rows, rows)
    block = back_ref[:, 16 * half : 16 * half + 16, :].reshape(chan, rows)
    turned = block.astype(F32).T
    mixed = mixed_ref[here, :].astype(F32)
    out_ref[...] = (query_ref[here, :] * (turned + skip_ref[...] * mixed)).astype(BF16)


def gate(back, mixed, query, skip, half):
    return pl.pallas_call(
        functools.partial(gate_kernel, half),
        out_shape=jax.ShapeDtypeStruct((back.shape[2], mixed.shape[1]), BF16),
        in_specs=[VMEM] * 4,
        out_specs=VMEM,
        compiler_params=pltpu.CompilerParams(vmem_limit_bytes=8 * MIB),
        name="gate%d" % half,
    )(back, mixed, query, skip)


def near_parts(pieces):
    me = lax.axis_index("tp")
    x, y = me // 2, me % 2
    offsets = [(0, 0), (0, 1), (-1, 0), (1, 0), (-1, 1), (1, 1)]
    rows = pieces[0].shape[0]
    parts = []
    for k, (dx, dy) in enumerate(offsets):
        there = ((x + dx + NX) % NX) * 2 + (y + dy) % 2
        parts.append((there, [(pieces[k], 0), (pieces[6 + k], rows)]))
    return parts


def far_parts(pieces):
    me = lax.axis_index("tp")
    x, y = me // 2, me % 2
    count = pieces[0].shape[0] // 2
    parts = []
    for dy in (0, 1):
        rows = pl.ds(dy * count, count)
        there = ((x + 2) % NX) * 2 + (y + dy) % 2
        sources = [(piece.at[rows], k * count) for k, piece in enumerate(pieces)]
        parts.append((there, sources))
    return parts


def output_kernel(parts_of, n_pieces, *refs):
    pieces, (weights, *start) = refs[:n_pieces], refs[n_pieces:-5]
    out_ref, act, wts, before, sem = refs[-5:]
    _, y, core = weight_slots()
    width = weights.shape[3]
    depth = wts.shape[1]
    copies = []
    for p, (there, sources) in enumerate(parts_of(pieces)):
        for src, first in sources:
            to = act.at[pl.ds(first, src.shape[0]), pl.ds(p * depth, depth)]
            copies.append(pltpu.make_async_copy(src, to, sem))
        for k in range(4):
            slot = ((y + k // 2) % 2) * 2 + (core + k % 2) % 2
            lanes = pl.ds(pl.multiple_of(slot * width, width), width)
            to = wts.at[p, :, lanes]
            copies.append(pltpu.make_async_copy(weights.at[there, k], to, sem))
    if start:
        copies.append(pltpu.make_async_copy(start[0], before, sem))
    for copy in copies:
        copy.start()
    for copy in copies:
        copy.wait()
    matrix = wts[...].reshape(-1, wts.shape[2])
    total = jnp.dot(act[...], matrix, preferred_element_type=F32)
    if start:
        total = total + before[...]
    out_ref[...] = total.astype(out_ref.dtype)


def output(pieces, parts_of, parts, weights, start, dtype):
    rows = 2 * pieces[0].shape[0]
    depth, width = weights.shape[2:]
    return pl.pallas_call(
        functools.partial(output_kernel, parts_of, len(pieces)),
        out_shape=jax.ShapeDtypeStruct((rows, 4 * width), dtype),
        in_specs=[HBM] * (len(pieces) + 1 + len(start)),
        out_specs=VMEM,
        scratch_shapes=[
            pltpu.VMEM((rows, parts * depth), BF16),
            pltpu.VMEM((parts, depth, 4 * width), BF16),
            pltpu.VMEM((rows, 4 * width) if start else (8, 128), F32),
            pltpu.SemaphoreType.DMA,
        ],
        compiler_params=pltpu.CompilerParams(vmem_limit_bytes=20 * MIB),
        name="output%d" % parts,
    )(*pieces, weights, *start)


def pair_ylo(own):
    return jnp.stack([own, swap_ylo(own)])


def local(tokens, w_in, short_taps, filters, skip, w_out):
    rows, _ = tokens.shape
    depth, chan = w_in.shape[1:]
    taps = short_taps.transpose(0, 2, 1)

    kv = jnp.concatenate([w_in[1:], filters.reshape(2, 16, -1)], axis=1)
    kv_mine = gather_z(pair_ylo(kv))
    route = []
    for z in range(NZ):
        for r in range(4):
            for j in range(TP):
                route.append(((4 * z + r) * TP + j, (4 * j + r) * TP + z))
    w_out = lax.ppermute(w_out, ("ctx", "tp"), route)
    pieces, w_out = gather_tp(tokens, w_out)
    tail = last_rows(pieces)
    tail = lax.ppermute(tail, "ctx", [(i, i + 1) for i in range(CTX - 1)])

    kv_mine, tail, *pieces = barrier(kv_mine, tail, *pieces)
    w_in, kv_mine = barrier(w_in, kv_mine)
    kv_other = swap_core(kv_mine)
    q_mine = gather_z(pair_ylo(w_in[:1]))
    mixed, blocks = project(
        pieces,
        tail,
        (kv_mine, kv_other),
        taps[1:],
        [
            jax.ShapeDtypeStruct((rows, chan), BF16),
            jax.ShapeDtypeStruct((CTX, 32, 256), BF16),
        ],
    )

    w_out, blocks = barrier(w_out, blocks)
    o_pair = jnp.stack([w_out, swap_core(w_out)])
    o_pair = jnp.concatenate([o_pair, swap_ylo(o_pair)])
    sent = lax.all_to_all(blocks, "ctx", 0, 0, tiled=True)
    table = toeplitz((kv_mine, kv_other))
    o_pair, sent, table = barrier(o_pair, sent, table)
    result = conv(sent.reshape(CTX * 32, 256), table)
    q_mine, o_pair, result = barrier(q_mine, o_pair, result)
    back = lax.all_to_all(result.reshape(CTX, 32, 256), "ctx", 0, 0, tiled=True)
    o_mine = gather_z(o_pair)
    (query,) = project(
        pieces,
        tail,
        (q_mine, swap_core(q_mine)),
        taps[:1],
        [jax.ShapeDtypeStruct((rows, chan), F32)],
    )
    gated = [gate(back, mixed, query, skip[None, :], half) for half in range(2)]

    first, second = gather_tp(gated[0])[0], gather_tp(gated[1])[0]
    total = output(first[:6] + second[:6], near_parts, 6, o_mine, [], F32)
    return output(first[6:] + second[6:], far_parts, 2, o_mine, [total], BF16)


def solution(mesh):
    return jax.shard_map(
        local,
        mesh=mesh,
        in_specs=(
            P("ctx", "tp"),
            P(None, "ctx", "tp"),
            P(None, "tp", None),
            P("tp", "ctx"),
            P("tp"),
            P("tp", "ctx"),
        ),
        out_specs=P("ctx", "tp"),
        check_vma=False,
    )
```
